512 devices in a mesh: narrow: 8 (over y, core), wide: 64 (over x, z).
Axes of the slice: x: 4, y: 4, z: 16, core: 2. Of those that a mesh axis runs over, the one named last changes fastest.
Arguments:
- u_real: bfloat16 [1024, 131072], P('narrow', 'wide'), may hold values from -0.01171875 to 0.01171875
- u_imag: bfloat16 [1024, 131072], P('narrow', 'wide'), may hold values from -0.01171875 to 0.01171875
- psi_real: bfloat16 [131072, 512], P('wide', 'narrow'), may hold values from -6 to 6
- psi_imag: bfloat16 [131072, 512], P('wide', 'narrow'), may hold values from -6 to 6
- kick_angle: float32 [512], P('narrow'), may hold values from 0.3 to 2.5
- excited: int32 [131072], P('wide'), may hold values from 0 to 12
Outputs:
- out_real: float32 [512, 1024], P('wide', 'narrow')
- out_imag: float32 [512, 1024], P('wide', 'narrow')
The draws below stay inside these ranges and needn't reach their ends.
All inputs are finite; a program needn't handle non-finite values.
Results may differ from the reference program's by a relative error of at most 0.0028.
Values may be sent and summed in bfloat16 or wider, within the bound.
A program may use at most 64 MiB of HBM per device.

```python
import math
import jax
import jax.numpy as jnp
from jax import lax

DIM = 131072
ROWS = 1024
STATES = 512
MOST_EXCITED = 12


def with_ends(array, rng, least, largest):
    extent = array.shape
    place = [jax.random.randint(jax.random.fold_in(rng, axis), (), 0, extent[axis]) for axis in range(len(extent))]
    array = array.at[tuple(place)].set(least)
    longest = extent.index(max(extent))
    place[longest] = (place[longest] + 1) % extent[longest]
    return array.at[tuple(place)].set(largest)


def steps_of(key, extent, cuts, low, high):
    level = 1.0
    for axis_at, parts in cuts:
        heights = jax.random.uniform(jax.random.fold_in(jax.random.fold_in(key, 6), axis_at), (parts,), jnp.float32, low / len(cuts), high / len(cuts))
        level = level * jnp.repeat(jnp.exp(heights), extent[axis_at] // parts).reshape((-1,) + (1,) * (len(extent) - 1 - axis_at))
    return level


def bell_draw(stream_key, dims, spread, reach, cuts=(), dtype=jnp.bfloat16):
    array = spread * jax.random.normal(stream_key, dims, jnp.float32)
    if cuts:
        array = array * steps_of(stream_key, dims, cuts, -0.22, 0.18)
    return jnp.clip(array, -reach, reach).astype(dtype)


def setup_inputs(seed: int = 0) -> dict:
    key_list = jax.random.split(jax.random.key(seed), 7)
    u_real = bell_draw(key_list[0], (ROWS, DIM), (2 * DIM) ** -0.5, 0.01171875, ((0, 8), (1, 64)))
    u_imag = bell_draw(key_list[1], (ROWS, DIM), (2 * DIM) ** -0.5, 0.01171875, ((0, 8), (1, 64)))
    psi_real = bell_draw(key_list[2], (DIM, STATES), 1.0, 6.0, ((0, 64), (1, 8)))
    psi_imag = bell_draw(key_list[3], (DIM, STATES), 1.0, 6.0, ((0, 64), (1, 8)))
    kick_angle = jnp.clip(jnp.exp(math.log(2.5) - 2.1202635 * jax.random.uniform(key_list[4], (STATES,), jnp.float32) ** steps_of(key_list[4], (STATES,), ((0, 8),), -0.2, 0.2)), 0.3, 2.5)
    excited = with_ends(jax.random.randint(key_list[5], (DIM,), 0, MOST_EXCITED + 1), jax.random.fold_in(key_list[5], 1), 0, MOST_EXCITED).astype(jnp.int32)
    return {"u_real": u_real, "u_imag": u_imag, "psi_real": psi_real, "psi_imag": psi_imag, "kick_angle": kick_angle, "excited": excited}


def apply_kick(psi_real, psi_imag, kick_angle, excited):
    phases = excited.astype(jnp.float32)[:, None] * kick_angle[None, :]
    cosine = jnp.cos(phases)
    sine = jnp.sin(phases)
    part_real = psi_real.astype(jnp.float32)
    part_imag = psi_imag.astype(jnp.float32)
    kicked_real = (cosine * part_real + sine * part_imag).astype(jnp.bfloat16)
    kicked_imag = (cosine * part_imag - sine * part_real).astype(jnp.bfloat16)
    return kicked_real, kicked_imag


def reference(u_real, u_imag, psi_real, psi_imag, kick_angle, excited):
    span_cols = min(DIM, 8192)
    blocks = DIM // span_cols
    contract = (((0,), (1,)), ((), ()))

    def step(position, totals):
        first_col = (position * span_cols).astype(jnp.int32)
        rows_real = lax.dynamic_slice_in_dim(u_real, first_col, span_cols, 1)
        rows_imag = lax.dynamic_slice_in_dim(u_imag, first_col, span_cols, 1)
        block_real = lax.dynamic_slice_in_dim(psi_real, first_col, span_cols, 0)
        block_imag = lax.dynamic_slice_in_dim(psi_imag, first_col, span_cols, 0)
        block_excited = lax.dynamic_slice_in_dim(excited, first_col, span_cols, 0)
        kicked_real, kicked_imag = apply_kick(block_real, block_imag, kick_angle, block_excited)
        rr = lax.dot_general(kicked_real, rows_real, contract, preferred_element_type=jnp.float32)
        ii = lax.dot_general(kicked_imag, rows_imag, contract, preferred_element_type=jnp.float32)
        ri = lax.dot_general(kicked_imag, rows_real, contract, preferred_element_type=jnp.float32)
        ir = lax.dot_general(kicked_real, rows_imag, contract, preferred_element_type=jnp.float32)
        return (totals[0] + rr - ii, totals[1] + ri + ir)

    empty = jnp.zeros((STATES, ROWS), jnp.float32)
    out_real, out_imag = lax.fori_loop(0, blocks, step, (empty, empty))
    return out_real, out_imag
```

```python
import jax
import jax.numpy as jnp
from jax import lax
from jax.experimental import pallas as pl
from jax.experimental.pallas import tpu as pltpu
from jax.sharding import Mesh
from jax.sharding import PartitionSpec as P

Y, C, X, Z = 4, 2, 4, 16
NARROW = ("y", "c")
WIDE = ("x", "z")
PIECE = 16
PIECES = 4
MESH = pl.DeviceIdType.MESH

OWN, UP, FAR, DOWN = 0, 1, 2, 3
UPWARD = (0, 1, 2, 3)
DOWNWARD = (2, 3, 0, 1)


def kernel(
    angle_hbm,
    excited_hbm,
    psi_real_hbm,
    psi_imag_hbm,
    u_real_hbm,
    u_imag_hbm,
    out_real_ref,
    out_imag_ref,
    angle,
    excited,
    psi,
    w,
    hot,
    table,
    kbuf,
    zsend,
    zbuf,
    xsend,
    xbuf,
    in_sem,
    u_sem,
    u_send,
    u_recv,
    y_send,
    y_recv,
    z_send,
    z_recv,
    x_send,
    x_recv,
):
    y, c, x, z = (lax.axis_index(a) for a in ("y", "c", "x", "z"))
    up, down = lax.rem(y + 1, Y), lax.rem(y + Y - 1, Y)
    half = z // 8
    summing = c == half
    depth = psi.shape[-1]

    barrier = pltpu.get_barrier_semaphore()

    def greet(**where):
        pl.semaphore_signal(barrier, inc=1, device_id=where, device_id_type=MESH)

    greet(y=up)
    greet(y=down)
    greet(c=1 - c)
    for d in range(1, X):
        greet(x=lax.rem(x + d, X), c=half)

    @pl.when(summing)
    def _():
        @pl.loop(1, Z)
        def _(d):
            greet(z=lax.rem(z + d, Z))

    loads = [
        pltpu.make_async_copy(angle_hbm, angle, in_sem.at[0]),
        pltpu.make_async_copy(excited_hbm, excited, in_sem.at[1]),
        pltpu.make_async_copy(psi_real_hbm, psi.at[0], in_sem.at[2]),
        pltpu.make_async_copy(psi_imag_hbm, psi.at[1], in_sem.at[3]),
        pltpu.make_async_copy(u_real_hbm, w.at[c, 0], u_sem.at[0]),
        pltpu.make_async_copy(u_imag_hbm, w.at[c, 1], u_sem.at[1]),
    ]
    for load in loads:
        load.start()

    loads[0].wait()
    number = lax.broadcasted_iota(jnp.int32, (PIECE, 64), 0).astype(jnp.float32)
    phases = number * angle[...]
    full = jnp.concatenate([jnp.cos(phases), jnp.sin(phases)], axis=1)
    high = full.astype(jnp.bfloat16).astype(jnp.float32)
    rest = full - high
    middle = rest.astype(jnp.bfloat16).astype(jnp.float32)
    low = rest - middle
    terms = jnp.concatenate([high, middle, low, jnp.zeros((128 - 3 * PIECE, 128), jnp.float32)], axis=0)
    table[...] = terms.T.astype(jnp.bfloat16)
    loads[1].wait()
    row = lax.broadcasted_iota(jnp.int32, (128, depth), 0) % PIECE
    hot[...] = jnp.where(row == excited[...], 1.0, 0.0).astype(jnp.bfloat16)
    loads[2].wait()
    loads[3].wait()

    def kick(j):
        at = slice(PIECE * j, PIECE * (j + 1))
        angles = jnp.concatenate([table[at, :], table[64 + PIECE * j : 64 + PIECE * (j + 1), :]], axis=0)
        turn = jnp.dot(angles, hot[...], preferred_element_type=jnp.float32)
        cosine, sine = turn[:PIECE], turn[PIECE:]
        real = psi[0, at, :].astype(jnp.float32)
        imag = psi[1, at, :].astype(jnp.float32)
        kbuf[OWN, j, :PIECE] = (cosine * real + sine * imag).astype(jnp.bfloat16)
        kbuf[OWN, j, PIECE:] = (cosine * imag - sine * real).astype(jnp.bfloat16)

    def to_y(source, j, slot, where):
        return pltpu.make_async_remote_copy(
            src_ref=kbuf.at[source, j],
            dst_ref=kbuf.at[slot, j],
            send_sem=y_send,
            recv_sem=y_recv.at[slot, j],
            device_id={"y": where},
            device_id_type=MESH,
        )

    def arrived(slot, j):
        to_y(slot, j, slot, up).wait_recv()

    kick(UPWARD[0])

    @pl.when(summing)
    def _():
        pl.semaphore_wait(barrier, 16)

    @pl.when(jnp.logical_not(summing))
    def _():
        pl.semaphore_wait(barrier, 11)

    to_y(OWN, UPWARD[0], DOWN, up).start()
    kick(DOWNWARD[0])
    to_y(OWN, DOWNWARD[0], UP, down).start()
    u_copies = [
        pltpu.make_async_remote_copy(
            src_ref=u,
            dst_ref=w.at[c, i],
            send_sem=u_send.at[i],
            recv_sem=u_recv.at[i],
            device_id={"c": 1 - c},
            device_id_type=MESH,
        )
        for i, u in enumerate((u_real_hbm, u_imag_hbm))
    ]
    for copy in u_copies:
        copy.start()
    kick(UPWARD[1])
    to_y(OWN, UPWARD[1], DOWN, up).start()
    kick(DOWNWARD[1])
    to_y(OWN, DOWNWARD[1], UP, down).start()
    for t in (2, 3):
        to_y(OWN, UPWARD[t], DOWN, up).start()
        to_y(OWN, DOWNWARD[t], UP, down).start()

    loads[4].wait()
    loads[5].wait()
    for i, u in enumerate((u_real_hbm, u_imag_hbm)):
        pltpu.make_async_remote_copy(
            src_ref=u,
            dst_ref=w.at[1 - c, i],
            send_sem=u_send.at[i],
            recv_sem=u_recv.at[i],
            device_id={"c": 1 - c},
            device_id_type=MESH,
        ).wait_recv()

    def to_z(slot, target):
        j = (target % 8) // 2
        return pltpu.make_async_remote_copy(
            src_ref=zsend.at[slot, j, target % 2],
            dst_ref=zbuf.at[slot, lax.rem(z - target + Z, Z)],
            send_sem=z_send,
            recv_sem=z_recv.at[slot],
            device_id={"z": target},
            device_id_type=MESH,
        )

    def multiply(slot, j):
        products = lax.dot_general(
            kbuf[slot, j],
            w[...].reshape(4 * 128, depth),
            (((1,), (1,)), ((), ())),
            preferred_element_type=jnp.float32,
        )
        by_real, by_imag = products[:PIECE], products[PIECE:]
        parts = []
        for r in range(C):
            at_real, at_imag = slice(256 * r, 256 * r + 128), slice(256 * r + 128, 256 * (r + 1))
            parts.append(
                (by_real[:, at_real] - by_imag[:, at_imag], by_imag[:, at_real] + by_real[:, at_imag])
            )
        for h in range(2):
            at = slice(8 * h, 8 * (h + 1))
            rows = [part[at] for r in range(C) for part in parts[r]]
            zsend[slot, j, h] = jnp.concatenate(rows, axis=0).astype(jnp.bfloat16)
        for h in range(2):
            target = 8 * c + 2 * j + h

            @pl.when(target != z)
            def _():
                to_z(slot, target).start()

    for j in range(PIECES):
        multiply(OWN, j)
    for t in range(PIECES):
        arrived(DOWN, UPWARD[t])
        if t < 2:
            to_y(DOWN, UPWARD[t], FAR, up).start()
        multiply(DOWN, UPWARD[t])
        arrived(UP, DOWNWARD[t])
        if t < 2:
            to_y(UP, DOWNWARD[t], FAR, down).start()
        multiply(UP, DOWNWARD[t])
    for t in range(2):
        arrived(FAR, UPWARD[t])
        multiply(FAR, UPWARD[t])
        arrived(FAR, DOWNWARD[t])
        multiply(FAR, DOWNWARD[t])

    def to_x(slot, r):
        owner = lax.rem(y + slot, Y)
        return owner, pltpu.make_async_remote_copy(
            src_ref=xsend.at[slot, pl.ds(16 * r, 16)],
            dst_ref=xbuf.at[lax.rem(x - owner + X, X)],
            send_sem=x_send,
            recv_sem=x_recv,
            device_id={"x": owner, "c": r},
            device_id_type=MESH,
        )

    @pl.when(summing)
    def _():
        for slot in (OWN, DOWN, UP, FAR):
            others = zbuf.at[slot, pl.ds(1, Z - 1)]
            pltpu.make_async_copy(others, others, z_recv.at[slot]).wait()
            total = zsend[slot, (z % 8) // 2, z % 2].astype(jnp.float32)
            for d in range(1, Z):
                total = total + zbuf[slot, d].astype(jnp.float32)
            xsend[slot] = total
            for r in range(C):
                owner, copy = to_x(slot, r)

                @pl.when(jnp.logical_or(owner != x, c != r))
                def _():
                    copy.start()

    def finish(total):
        out_real_ref[...] = total[:8]
        out_imag_ref[...] = total[8:]

    @pl.when(summing)
    def _():
        others = xbuf.at[pl.ds(1, X - 1)]
        pltpu.make_async_copy(others, others, x_recv).wait()
        mine = xsend[lax.rem(x - y + Y, Y), pl.ds(pl.multiple_of(16 * c, 16), 16)]
        finish(mine + xbuf[1] + xbuf[2] + xbuf[3])

    @pl.when(jnp.logical_not(summing))
    def _():
        pltpu.make_async_copy(xbuf, xbuf, x_recv).wait()
        finish(xbuf[0] + xbuf[1] + xbuf[2] + xbuf[3])

    for copy in u_copies:
        copy.wait_send()
    sent = kbuf.at[pl.ds(0, 3)]
    pltpu.make_async_copy(sent, sent, y_send).wait()

    @pl.when(summing)
    def _():
        for sent, sem in ((zbuf.at[pl.ds(0, 4), pl.ds(0, 7)], z_send), (xsend.at[pl.ds(0, 3)], x_send), (xsend.at[3, pl.ds(0, 16)], x_send)):
            pltpu.make_async_copy(sent, sent, sem).wait()

    @pl.when(jnp.logical_not(summing))
    def _():
        sent = zbuf.at[pl.ds(0, 4), pl.ds(0, 8)]
        pltpu.make_async_copy(sent, sent, z_send).wait()


def on_device(u_real, u_imag, psi_real, psi_imag, kick_angle, excited):
    rows, depth = u_real.shape
    bf16, f32 = jnp.bfloat16, jnp.float32
    any_place = pl.BlockSpec(memory_space=pl.ANY)
    vmem = pl.BlockSpec(memory_space=pltpu.VMEM)
    dma = pltpu.SemaphoreType.DMA
    return pl.pallas_call(
        kernel,
        out_shape=(jax.ShapeDtypeStruct((8, rows), f32),) * 2,
        in_specs=[any_place] * 6,
        out_specs=(vmem, vmem),
        scratch_shapes=[
            pltpu.VMEM((1, 64), f32),
            pltpu.VMEM((1, depth), jnp.int32),
            pltpu.VMEM((2, 64, depth), bf16),
            pltpu.VMEM((C, 2, rows, depth), bf16),
            pltpu.VMEM((128, depth), bf16),
            pltpu.VMEM((128, 128), bf16),
            pltpu.VMEM((Y, PIECES, 2 * PIECE, depth), bf16),
            pltpu.VMEM((Y, PIECES, 2, 32, 128), bf16),
            pltpu.VMEM((Y, Z, 32, 128), bf16),
            pltpu.VMEM((Y, 32, 128), f32),
            pltpu.VMEM((X, 16, 128), f32),
            dma((4,)),
            dma((2,)),
            dma((2,)),
            dma((2,)),
            dma,
            dma((Y, PIECES)),
            dma,
            dma((Y,)),
            dma,
            dma,
        ],
        compiler_params=pltpu.CompilerParams(
            collective_id=0, has_side_effects=True, vmem_limit_bytes=56 << 20
        ),
        cost_estimate=pl.CostEstimate(
            flops=4 * 2 * 256 * 256 * depth, bytes_accessed=6 * rows * depth * 2, transcendentals=0
        ),
    )(kick_angle[None, :], excited[None, :], psi_real.T, psi_imag.T, u_real, u_imag)


def solution(mesh):
    split = Mesh(mesh.devices.reshape(Y, C, X, Z), ("y", "c", "x", "z"))
    return jax.shard_map(
        on_device,
        mesh=split,
        in_specs=(
            P(NARROW, WIDE),
            P(NARROW, WIDE),
            P(WIDE, NARROW),
            P(WIDE, NARROW),
            P(NARROW),
            P(WIDE),
        ),
        out_specs=(P(WIDE, NARROW), P(WIDE, NARROW)),
        check_vma=False,
    )
```

```python
import jax
import jax.numpy as jnp
from jax import lax
from jax.experimental import pallas as pl
from jax.experimental.pallas import tpu as pltpu
from jax.sharding import Mesh
from jax.sharding import PartitionSpec as P

Y, C, X, Z = 4, 2, 4, 16
NARROW = ("y", "c")
WIDE = ("x", "z")
PIECE = 16
PIECES = 4
MESH = pl.DeviceIdType.MESH

OWN, UP, FAR, DOWN = 0, 1, 2, 3
PLACE = {FAR: 0, UP: 1, DOWN: 2}
EARLY = 4
HELLO, RELAY, ACROSS, Y_KNOWN, X_KNOWN, Z_KNOWN = range(6)
PAIRS = ((0, 2, 4, 5), (7, 1, 3, 6))
CORE_OF = tuple(0 if k in PAIRS[0] else 1 for k in range(Z // 2))
NUMBER_OF = tuple(PAIRS[CORE_OF[k]].index(k) for k in range(Z // 2))
KEPT = tuple([(k % 4, p) for p, k in enumerate(PAIRS[c]) if k // 4 == c] for c in range(C))
GIVEN = tuple([(k % 4, p) for p, k in enumerate(PAIRS[1 - c]) if k // 4 == c] for c in range(C))


def kernel(
    angle_hbm,
    excited_hbm,
    psi_real_hbm,
    psi_imag_hbm,
    u_real_hbm,
    u_imag_hbm,
    out_ref,
    angle,
    excited,
    psi,
    w,
    hot,
    table,
    own,
    given,
    kbuf,
    xsend,
    xin,
    zsend,
    zbuf,
    in_sem,
    u_sem,
    u_send,
    u_recv,
    give_send,
    give_recv,
    y_send,
    y_recv,
    x_send,
    x_recv,
    z_send,
    z_recv,
    known,
):
    y, c, x, z = (lax.axis_index(a) for a in ("y", "c", "x", "z"))
    up, down = lax.rem(y + 1, Y), lax.rem(y + Y - 1, Y)
    pair_of_z = z // 2
    core_of_z = sum(jnp.where(pair_of_z == k, CORE_OF[k], 0) for k in range(Z // 2))
    number_of_z = sum(jnp.where(pair_of_z == k, NUMBER_OF[k], 0) for k in range(Z // 2))

    def by_core(values):
        return jnp.where(c == 0, values[0], values[1])

    mine = lax.rem(x - y + Y, Y)
    depth = psi.shape[-1]

    barrier = pltpu.get_barrier_semaphore()

    def greet(**where):
        pl.semaphore_signal(barrier, inc=1, device_id=where, device_id_type=MESH)

    @pl.when(c == 0)
    def _():
        greet(y=up)
        greet(y=down)
        for d in (1, X - 1):
            greet(x=lax.rem(x + d, X))

    @pl.when(c == 1)
    def _():
        greet(c=0)


    loads = [
        pltpu.make_async_copy(angle_hbm, angle, in_sem.at[0]),
        pltpu.make_async_copy(excited_hbm, excited, in_sem.at[1]),
        pltpu.make_async_copy(psi_real_hbm, psi.at[0], in_sem.at[2]),
        pltpu.make_async_copy(psi_imag_hbm, psi.at[1], in_sem.at[3]),
        pltpu.make_async_copy(u_real_hbm, w.at[c, 0], u_sem.at[0]),
        pltpu.make_async_copy(u_imag_hbm, w.at[c, 1], u_sem.at[1]),
    ]
    for load in loads:
        load.start()

    @pl.loop(1, Z)
    def _(d):
        greet(z=lax.rem(z + d, Z), c=1)

    def tell(what, **where):
        pl.semaphore_signal(known.at[what], inc=1, device_id=where, device_id_type=MESH)

    loads[0].wait()
    number = lax.broadcasted_iota(jnp.int32, (PIECE, 64), 0).astype(jnp.float32)
    phases = number * angle[...]
    full = jnp.concatenate([jnp.cos(phases), jnp.sin(phases)], axis=1)
    high = full.astype(jnp.bfloat16).astype(jnp.float32)
    rest = full - high
    middle = rest.astype(jnp.bfloat16).astype(jnp.float32)
    low = rest - middle
    terms = jnp.concatenate([high, middle, low, jnp.zeros((128 - 3 * PIECE, 128), jnp.float32)], axis=0)
    table[...] = terms.T.astype(jnp.bfloat16)
    loads[1].wait()
    row = lax.broadcasted_iota(jnp.int32, (128, depth), 0) % PIECE
    hot[...] = jnp.where(row == excited[...], 1.0, 0.0).astype(jnp.bfloat16)
    loads[2].wait()
    loads[3].wait()

    def kick(place, to):
        at = pl.ds(pl.multiple_of(PIECE * place, PIECE), PIECE)
        sines_at = pl.ds(pl.multiple_of(64 + PIECE * place, PIECE), PIECE)
        angles = jnp.concatenate([table[at, :], table[sines_at, :]], axis=0)
        turn = jnp.dot(angles, hot[...], preferred_element_type=jnp.float32)
        cosine, sine = turn[:PIECE], turn[PIECE:]
        real = psi[0, at, :].astype(jnp.float32)
        imag = psi[1, at, :].astype(jnp.float32)
        to[:PIECE] = (cosine * real + sine * imag).astype(jnp.bfloat16)
        to[PIECE:] = (cosine * imag - sine * real).astype(jnp.bfloat16)

    def keep(i):
        kick(by_core([KEPT[k][i][0] for k in range(C)]), own.at[by_core([KEPT[k][i][1] for k in range(C)])])

    def give(i):
        kick(by_core([GIVEN[k][i][0] for k in range(C)]), given.at[i])
        number = by_core([GIVEN[k][i][1] for k in range(C)])
        pltpu.make_async_remote_copy(
            src_ref=given.at[i],
            dst_ref=own.at[number],
            send_sem=give_send,
            recv_sem=give_recv.at[number],
            device_id={"c": 1 - c},
            device_id_type=MESH,
        ).start()

    def was_given(j):
        for k in range(C):
            if j in [p for _, p in GIVEN[1 - k]]:

                @pl.when(c == k)
                def _():
                    pltpu.make_async_copy(own.at[j], own.at[j], give_recv.at[j]).wait()

    def own_to(j, slot, where):
        return pltpu.make_async_remote_copy(
            src_ref=own.at[j],
            dst_ref=kbuf.at[j, PLACE[slot]],
            send_sem=y_send,
            recv_sem=y_recv.at[slot, j],
            device_id={"y": where},
            device_id_type=MESH,
        )

    def send_own(j):
        own_to(j, DOWN, up).start()
        own_to(j, UP, down).start()

    def pass_on(slot, j):
        part = pl.ds(0, PIECE) if slot == DOWN else pl.ds(PIECE, PIECE)
        pltpu.make_async_remote_copy(
            src_ref=kbuf.at[j, PLACE[slot], part],
            dst_ref=kbuf.at[j, PLACE[FAR], part],
            send_sem=y_send,
            recv_sem=y_recv.at[FAR, j],
            device_id={"y": up if slot == DOWN else down},
            device_id_type=MESH,
        ).start()

    def arrived(slot, j):
        own_to(j, slot, up).wait_recv()

    def pair_arrived(j):
        arrived(DOWN, j)
        pass_on(DOWN, j)
        arrived(UP, j)
        pass_on(UP, j)

    keep(0)
    @pl.when(c == 0)
    def _():
        pl.semaphore_wait(barrier, 5)
        send_own(0)
        tell(HELLO, c=1)
        tell(RELAY, y=up)
        tell(RELAY, y=down)
        for d in (1, X - 1):
            tell(RELAY, x=lax.rem(x + d, X))

    @pl.when(c == 1)
    def _():
        pl.semaphore_wait(known.at[HELLO], 1)

    u_copies = [
        pltpu.make_async_remote_copy(
            src_ref=u,
            dst_ref=w.at[c, i],
            send_sem=u_send.at[i],
            recv_sem=u_recv.at[i],
            device_id={"c": 1 - c},
            device_id_type=MESH,
        )
        for i, u in enumerate((u_real_hbm, u_imag_hbm))
    ]
    give(0)
    give(1)
    for copy in u_copies:
        copy.start()
    keep(1)

    @pl.when(c == 0)
    def _():
        send_own(1)
        pl.semaphore_wait(known.at[RELAY], 4)
        tell(Y_KNOWN, c=1)
        tell(ACROSS, x=lax.rem(x + 2, X))

    @pl.when(c == 1)
    def _():
        pl.semaphore_wait(known.at[Y_KNOWN], 1)
        send_own(0)

    was_given(1)
    pl.when(c == 1)(lambda: send_own(1))
    was_given(2)
    send_own(2)
    pair_arrived(0)
    was_given(3)
    send_own(3)

    loads[4].wait()
    loads[5].wait()
    for i, u in enumerate((u_real_hbm, u_imag_hbm)):
        pltpu.make_async_remote_copy(
            src_ref=u,
            dst_ref=w.at[1 - c, i],
            send_sem=u_send.at[i],
            recv_sem=u_recv.at[i],
            device_id={"c": 1 - c},
            device_id_type=MESH,
        ).wait_recv()

    def multiply(states, pieces):
        products = lax.dot_general(
            states,
            w[...].reshape(4 * 128, depth),
            (((1,), (1,)), ((), ())),
            preferred_element_type=jnp.float32,
        )
        for i, (slot, j) in enumerate(pieces):
            by_real = products[2 * PIECE * i : 2 * PIECE * i + PIECE]
            by_imag = products[2 * PIECE * i + PIECE : 2 * PIECE * (i + 1)]
            parts = []
            for r in range(C):
                at_real, at_imag = slice(256 * r, 256 * r + 128), slice(256 * r + 128, 256 * (r + 1))
                parts.append(by_real[:, at_real] - by_imag[:, at_imag])
                parts.append(by_imag[:, at_real] + by_real[:, at_imag])
            xsend[slot, j] = jnp.concatenate(
                [part[8 * h : 8 * (h + 1)] for h in range(2) for part in parts], axis=0
            ).astype(jnp.bfloat16)

            @pl.when(slot != mine)
            def _():
                owner = lax.rem(y + slot, Y)
                pltpu.make_async_remote_copy(
                    src_ref=xsend.at[slot, j],
                    dst_ref=xin.at[j, lax.rem(x - owner + X, X) - 1],
                    send_sem=x_send,
                    recv_sem=x_recv.at[j],
                    device_id={"x": owner},
                    device_id_type=MESH,
                ).start()

    def sum_over_x(slot, j):
        @pl.when(slot == mine)
        def _():
            pltpu.make_async_copy(xin.at[j], xin.at[j], x_recv.at[j]).wait()
            total = xsend[slot, j].astype(jnp.float32)
            for d in range(X - 1):
                total = total + xin[j, d].astype(jnp.float32)
            zsend[j] = total.astype(jnp.bfloat16)
            for h in range(2):
                target = 2 * by_core([PAIRS[k][j] for k in range(C)]) + h
                for r in range(C):

                    @pl.when(jnp.logical_or(target != z, c != r))
                    def _():
                        pltpu.make_async_remote_copy(
                            src_ref=zsend.at[j, pl.ds(32 * h + 16 * r, 16)],
                            dst_ref=zbuf.at[lax.rem(z - target + Z, Z)],
                            send_sem=z_send,
                            recv_sem=z_recv,
                            device_id={"z": target, "c": r},
                            device_id_type=MESH,
                        ).start()

    def pair(j):
        multiply(kbuf[j, 1:3].reshape(4 * PIECE, depth), [(UP, j), (DOWN, j)])

    def far(j):
        arrived(FAR, j)
        multiply(kbuf[j, 0], [(FAR, j)])

    @pl.when(c == 0)
    def _():
        pl.semaphore_wait(known.at[ACROSS], 1)
        tell(X_KNOWN, c=1)

    @pl.when(c == 1)
    def _():
        pl.semaphore_wait(known.at[X_KNOWN], 1)

    multiply(own[...].reshape(8 * PIECE, depth), [(OWN, j) for j in range(PIECES)])

    pair(0)

    def know_z():
        @pl.when(c == 1)
        def _():
            pl.semaphore_wait(barrier, 2 * (Z - 1))
            tell(Z_KNOWN, c=0)

        @pl.when(c == 0)
        def _():
            pl.semaphore_wait(known.at[Z_KNOWN], 1)

    def sums(*which):
        for slot, j in which:
            sum_over_x(slot, j)

    early = z < EARLY

    def first_sums():
        sums((OWN, 0), (UP, 0), (DOWN, 0), (OWN, 1))

    def second_sums():
        sums((FAR, 0), (UP, 1), (DOWN, 1), (OWN, 2), (OWN, 3))

    pair_arrived(1)
    pair(1)
    far(0)
    pair_arrived(2)

    @pl.when(jnp.logical_not(early))
    def _():
        know_z()
        first_sums()

    pair(2)
    far(1)
    pair_arrived(3)

    @pl.when(jnp.logical_not(early))
    def _():
        second_sums()

    pair(3)

    @pl.when(early)
    def _():
        know_z()
        first_sums()
        second_sums()

    far(2)
    sums((UP, 2), (DOWN, 2), (FAR, 1))
    far(3)
    sums((UP, 3), (DOWN, 3), (FAR, 2), (FAR, 3))

    @pl.when(c == core_of_z)
    def _():
        others = zbuf.at[pl.ds(1, Z - 1)]
        pltpu.make_async_copy(others, others, z_recv).wait()
        here = 32 * (z % 2) + 16 * c
        total = zsend[number_of_z, pl.ds(pl.multiple_of(here, 16), 16)].astype(jnp.float32)
        for d in range(1, Z):
            total = total + zbuf[d].astype(jnp.float32)
        out_ref[...] = total

    @pl.when(c != core_of_z)
    def _():
        pltpu.make_async_copy(zbuf, zbuf, z_recv).wait()
        total = zbuf[0].astype(jnp.float32)
        for d in range(1, Z):
            total = total + zbuf[d].astype(jnp.float32)
        out_ref[...] = total

    for copy in u_copies:
        copy.wait_send()
    pltpu.make_async_copy(given, given, give_send).wait()
    pltpu.make_async_copy(kbuf, kbuf, y_send).wait()
    pltpu.make_async_copy(xin, xin, x_send).wait()

    @pl.when(c == core_of_z)
    def _():
        sent = zbuf.at[pl.ds(1, Z - 1)]
        pltpu.make_async_copy(sent, sent, z_send).wait()

    @pl.when(c != core_of_z)
    def _():
        pltpu.make_async_copy(zbuf, zbuf, z_send).wait()


def on_device(u_real, u_imag, psi_real, psi_imag, kick_angle, excited):
    rows, depth = u_real.shape
    bf16, f32 = jnp.bfloat16, jnp.float32
    any_place = pl.BlockSpec(memory_space=pl.ANY)
    vmem = pl.BlockSpec(memory_space=pltpu.VMEM)
    dma = pltpu.SemaphoreType.DMA
    out = pl.pallas_call(
        kernel,
        out_shape=jax.ShapeDtypeStruct((16, rows), f32),
        in_specs=[any_place] * 6,
        out_specs=vmem,
        scratch_shapes=[
            pltpu.VMEM((1, 64), f32),
            pltpu.VMEM((1, depth), jnp.int32),
            pltpu.VMEM((2, 64, depth), bf16),
            pltpu.VMEM((C, 2, rows, depth), bf16),
            pltpu.VMEM((128, depth), bf16),
            pltpu.VMEM((128, 128), bf16),
            pltpu.VMEM((PIECES, 2 * PIECE, depth), bf16),
            pltpu.VMEM((2, 2 * PIECE, depth), bf16),
            pltpu.VMEM((PIECES, 3, 2 * PIECE, depth), bf16),
            pltpu.VMEM((Y, PIECES, 64, rows), bf16),
            pltpu.VMEM((PIECES, X - 1, 64, rows), bf16),
            pltpu.VMEM((PIECES, 64, rows), bf16),
            pltpu.VMEM((Z, 16, rows), bf16),
            dma((4,)),
            dma((2,)),
            dma((2,)),
            dma((2,)),
            dma,
            dma((PIECES,)),
            dma,
            dma((Y, PIECES)),
            dma,
            dma((PIECES,)),
            dma,
            dma,
            pltpu.SemaphoreType.REGULAR((6,)),
        ],
        compiler_params=pltpu.CompilerParams(
            collective_id=0, has_side_effects=True, vmem_limit_bytes=56 << 20
        ),
        cost_estimate=pl.CostEstimate(
            flops=4 * 2 * 256 * 256 * depth, bytes_accessed=6 * rows * depth * 2, transcendentals=0
        ),
    )(kick_angle[None, :], excited[None, :], psi_real.T, psi_imag.T, u_real, u_imag)
    return out[:8], out[8:]


def solution(mesh):
    split = Mesh(mesh.devices.reshape(Y, C, X, Z), ("y", "c", "x", "z"))
    return jax.shard_map(
        on_device,
        mesh=split,
        in_specs=(
            P(NARROW, WIDE),
            P(NARROW, WIDE),
            P(WIDE, NARROW),
            P(WIDE, NARROW),
            P(NARROW),
            P(WIDE),
        ),
        out_specs=(P(WIDE, NARROW), P(WIDE, NARROW)),
        check_vma=False,
    )
```

```python
import jax
import jax.numpy as jnp
from jax import lax
from jax.experimental import pallas as pl
from jax.experimental.pallas import tpu as pltpu
from jax.sharding import Mesh
from jax.sharding import PartitionSpec as P

Y, C, X, Z = 4, 2, 4, 16
NARROW = ("y", "c")
WIDE = ("x", "z")
PIECE = 16
PIECES = 4
MESH = pl.DeviceIdType.MESH

OWN, UP, FAR, DOWN = 0, 1, 2, 3
PLACE = {FAR: 0, UP: 1, DOWN: 2}
EARLY = 4
HELLO, RELAY, ACROSS, Y_KNOWN, X_KNOWN, Z_KNOWN = range(6)
PAIRS = ((0, 2, 4, 5), (1, 3, 7, 6))
CORE_OF = tuple(0 if k in PAIRS[0] else 1 for k in range(Z // 2))
NUMBER_OF = tuple(PAIRS[CORE_OF[k]].index(k) for k in range(Z // 2))
KEPT = tuple([(k % 4, p) for p, k in enumerate(PAIRS[c]) if k // 4 == c] for c in range(C))
GIVEN = tuple([(k % 4, p) for p, k in enumerate(PAIRS[1 - c]) if k // 4 == c] for c in range(C))


def kernel(
    angle_hbm,
    excited_hbm,
    psi_real_hbm,
    psi_imag_hbm,
    u_real_hbm,
    u_imag_hbm,
    out_ref,
    angle,
    excited,
    psi,
    w,
    hot,
    table,
    own,
    given,
    kbuf,
    xsend,
    xin,
    zsend,
    zbuf,
    in_sem,
    u_sem,
    u_send,
    u_recv,
    give_send,
    give_recv,
    y_send,
    y_recv,
    x_send,
    x_recv,
    z_send,
    z_recv,
    known,
):
    y, c, x, z = (lax.axis_index(a) for a in ("y", "c", "x", "z"))
    up, down = lax.rem(y + 1, Y), lax.rem(y + Y - 1, Y)
    pair_of_z = z // 2
    core_of_z = sum(jnp.where(pair_of_z == k, CORE_OF[k], 0) for k in range(Z // 2))
    number_of_z = sum(jnp.where(pair_of_z == k, NUMBER_OF[k], 0) for k in range(Z // 2))

    def by_core(values):
        return jnp.where(c == 0, values[0], values[1])

    mine = lax.rem(x - y + Y, Y)
    depth = psi.shape[-1]

    barrier = pltpu.get_barrier_semaphore()

    def greet(**where):
        pl.semaphore_signal(barrier, inc=1, device_id=where, device_id_type=MESH)

    @pl.when(c == 0)
    def _():
        greet(y=up)
        greet(y=down)
        for d in (1, X - 1):
            greet(x=lax.rem(x + d, X))

    @pl.when(c == 1)
    def _():
        greet(c=0)


    loads = [
        pltpu.make_async_copy(angle_hbm, angle, in_sem.at[0]),
        pltpu.make_async_copy(excited_hbm, excited, in_sem.at[1]),
        pltpu.make_async_copy(psi_real_hbm, psi.at[0], in_sem.at[2]),
        pltpu.make_async_copy(psi_imag_hbm, psi.at[1], in_sem.at[3]),
        pltpu.make_async_copy(u_real_hbm, w.at[c, 0], u_sem.at[0]),
        pltpu.make_async_copy(u_imag_hbm, w.at[c, 1], u_sem.at[1]),
    ]
    for load in loads:
        load.start()

    @pl.loop(1, Z)
    def _(d):
        greet(z=lax.rem(z + d, Z), c=1)

    def tell(what, **where):
        pl.semaphore_signal(known.at[what], inc=1, device_id=where, device_id_type=MESH)

    loads[0].wait()
    number = lax.broadcasted_iota(jnp.int32, (PIECE, 64), 0).astype(jnp.float32)
    phases = number * angle[...]
    full = jnp.concatenate([jnp.cos(phases), jnp.sin(phases)], axis=1)
    high = full.astype(jnp.bfloat16).astype(jnp.float32)
    rest = full - high
    middle = rest.astype(jnp.bfloat16).astype(jnp.float32)
    low = rest - middle
    terms = jnp.concatenate([high, middle, low, jnp.zeros((128 - 3 * PIECE, 128), jnp.float32)], axis=0)
    table[...] = terms.T.astype(jnp.bfloat16)
    loads[1].wait()
    row = lax.broadcasted_iota(jnp.int32, (128, depth), 0) % PIECE
    hot[...] = jnp.where(row == excited[...], 1.0, 0.0).astype(jnp.bfloat16)
    loads[2].wait()
    loads[3].wait()

    def kick(place, to):
        at = pl.ds(pl.multiple_of(PIECE * place, PIECE), PIECE)
        sines_at = pl.ds(pl.multiple_of(64 + PIECE * place, PIECE), PIECE)
        angles = jnp.concatenate([table[at, :], table[sines_at, :]], axis=0)
        turn = jnp.dot(angles, hot[...], preferred_element_type=jnp.float32)
        cosine, sine = turn[:PIECE], turn[PIECE:]
        real = psi[0, at, :].astype(jnp.float32)
        imag = psi[1, at, :].astype(jnp.float32)
        to[:PIECE] = (cosine * real + sine * imag).astype(jnp.bfloat16)
        to[PIECE:] = (cosine * imag - sine * real).astype(jnp.bfloat16)

    def keep(i):
        kick(by_core([KEPT[k][i][0] for k in range(C)]), own.at[by_core([KEPT[k][i][1] for k in range(C)])])

    def give(i):
        kick(by_core([GIVEN[k][i][0] for k in range(C)]), given.at[i])
        number = by_core([GIVEN[k][i][1] for k in range(C)])
        pltpu.make_async_remote_copy(
            src_ref=given.at[i],
            dst_ref=own.at[number],
            send_sem=give_send,
            recv_sem=give_recv.at[number],
            device_id={"c": 1 - c},
            device_id_type=MESH,
        ).start()

    def was_given(j):
        for k in range(C):
            if j in [p for _, p in GIVEN[1 - k]]:

                @pl.when(c == k)
                def _():
                    pltpu.make_async_copy(own.at[j], own.at[j], give_recv.at[j]).wait()

    def own_to(j, slot, where):
        return pltpu.make_async_remote_copy(
            src_ref=own.at[j],
            dst_ref=kbuf.at[j, PLACE[slot]],
            send_sem=y_send,
            recv_sem=y_recv.at[slot, j],
            device_id={"y": where},
            device_id_type=MESH,
        )

    def send_own(j):
        own_to(j, DOWN, up).start()
        own_to(j, UP, down).start()

    def pass_on(slot, j):
        part = pl.ds(0, PIECE) if slot == DOWN else pl.ds(PIECE, PIECE)
        pltpu.make_async_remote_copy(
            src_ref=kbuf.at[j, PLACE[slot], part],
            dst_ref=kbuf.at[j, PLACE[FAR], part],
            send_sem=y_send,
            recv_sem=y_recv.at[FAR, j],
            device_id={"y": up if slot == DOWN else down},
            device_id_type=MESH,
        ).start()

    def arrived(slot, j):
        own_to(j, slot, up).wait_recv()

    def pair_arrived(j):
        arrived(DOWN, j)
        pass_on(DOWN, j)
        arrived(UP, j)
        pass_on(UP, j)

    keep(0)
    @pl.when(c == 0)
    def _():
        pl.semaphore_wait(barrier, 5)
        send_own(0)
        tell(HELLO, c=1)
        tell(RELAY, y=up)
        tell(RELAY, y=down)
        for d in (1, X - 1):
            tell(RELAY, x=lax.rem(x + d, X))

    @pl.when(c == 1)
    def _():
        pl.semaphore_wait(known.at[HELLO], 1)

    u_copies = [
        pltpu.make_async_remote_copy(
            src_ref=u,
            dst_ref=w.at[c, i],
            send_sem=u_send.at[i],
            recv_sem=u_recv.at[i],
            device_id={"c": 1 - c},
            device_id_type=MESH,
        )
        for i, u in enumerate((u_real_hbm, u_imag_hbm))
    ]
    give(0)
    give(1)
    for copy in u_copies:
        copy.start()
    keep(1)

    @pl.when(c == 0)
    def _():
        send_own(1)
        pl.semaphore_wait(known.at[RELAY], 4)
        tell(Y_KNOWN, c=1)
        tell(ACROSS, x=lax.rem(x + 2, X))

    @pl.when(c == 1)
    def _():
        pl.semaphore_wait(known.at[Y_KNOWN], 1)

    was_given(0)
    pl.when(c == 1)(lambda: send_own(0))
    was_given(1)
    pl.when(c == 1)(lambda: send_own(1))
    was_given(2)
    pair_arrived(0)
    send_own(2)
    was_given(3)

    loads[4].wait()
    loads[5].wait()
    for i, u in enumerate((u_real_hbm, u_imag_hbm)):
        pltpu.make_async_remote_copy(
            src_ref=u,
            dst_ref=w.at[1 - c, i],
            send_sem=u_send.at[i],
            recv_sem=u_recv.at[i],
            device_id={"c": 1 - c},
            device_id_type=MESH,
        ).wait_recv()

    def multiply(states, pieces):
        products = lax.dot_general(
            states,
            w[...].reshape(4 * 128, depth),
            (((1,), (1,)), ((), ())),
            preferred_element_type=jnp.float32,
        )
        for i, (slot, j) in enumerate(pieces):
            by_real = products[2 * PIECE * i : 2 * PIECE * i + PIECE]
            by_imag = products[2 * PIECE * i + PIECE : 2 * PIECE * (i + 1)]
            parts = []
            for r in range(C):
                at_real, at_imag = slice(256 * r, 256 * r + 128), slice(256 * r + 128, 256 * (r + 1))
                parts.append(by_real[:, at_real] - by_imag[:, at_imag])
                parts.append(by_imag[:, at_real] + by_real[:, at_imag])
            xsend[slot, j] = jnp.concatenate(
                [part[8 * h : 8 * (h + 1)] for h in range(2) for part in parts], axis=0
            ).astype(jnp.bfloat16)

            @pl.when(slot != mine)
            def _():
                owner = lax.rem(y + slot, Y)
                pltpu.make_async_remote_copy(
                    src_ref=xsend.at[slot, j],
                    dst_ref=xin.at[j, lax.rem(x - owner + X, X) - 1],
                    send_sem=x_send,
                    recv_sem=x_recv.at[j],
                    device_id={"x": owner},
                    device_id_type=MESH,
                ).start()

    def sum_over_x(slot, j):
        @pl.when(slot == mine)
        def _():
            pltpu.make_async_copy(xin.at[j], xin.at[j], x_recv.at[j]).wait()
            total = xsend[slot, j].astype(jnp.float32)
            for d in range(X - 1):
                total = total + xin[j, d].astype(jnp.float32)
            zsend[j] = total.astype(jnp.bfloat16)
            for h in range(2):
                target = 2 * by_core([PAIRS[k][j] for k in range(C)]) + h
                for r in range(C):

                    @pl.when(jnp.logical_or(target != z, c != r))
                    def _():
                        pltpu.make_async_remote_copy(
                            src_ref=zsend.at[j, pl.ds(32 * h + 16 * r, 16)],
                            dst_ref=zbuf.at[lax.rem(z - target + Z, Z)],
                            send_sem=z_send,
                            recv_sem=z_recv,
                            device_id={"z": target, "c": r},
                            device_id_type=MESH,
                        ).start()

    def pair(j):
        multiply(kbuf[j, 1:3].reshape(4 * PIECE, depth), [(UP, j), (DOWN, j)])

    def far(j):
        arrived(FAR, j)
        multiply(kbuf[j, 0], [(FAR, j)])

    @pl.when(c == 0)
    def _():
        pl.semaphore_wait(known.at[ACROSS], 1)
        tell(X_KNOWN, c=1)

    @pl.when(c == 1)
    def _():
        pl.semaphore_wait(known.at[X_KNOWN], 1)

    multiply(own[...].reshape(8 * PIECE, depth), [(OWN, j) for j in range(PIECES)])

    pair(0)

    def know_z():
        @pl.when(c == 1)
        def _():
            pl.semaphore_wait(barrier, 2 * (Z - 1))
            tell(Z_KNOWN, c=0)

        @pl.when(c == 0)
        def _():
            pl.semaphore_wait(known.at[Z_KNOWN], 1)

    def sums(*which):
        for slot, j in which:
            sum_over_x(slot, j)

    early = z < EARLY

    def first_sums():
        sums((OWN, 0), (UP, 0), (DOWN, 0))

    def second_sums():
        sums((FAR, 0))

    def third_sums():
        sums((OWN, 1), (UP, 1), (DOWN, 1), (OWN, 2), (OWN, 3))

    pair_arrived(1)
    send_own(3)
    far(0)
    pair(1)

    @pl.when(jnp.logical_not(early))
    def _():
        know_z()
        first_sums()

    pair_arrived(2)

    @pl.when(jnp.logical_not(early))
    def _():
        second_sums()

    pair(2)
    far(1)
    pair_arrived(3)

    @pl.when(jnp.logical_not(early))
    def _():
        third_sums()

    pair(3)

    @pl.when(early)
    def _():
        know_z()
        first_sums()
        second_sums()
        third_sums()

    far(2)
    sums((UP, 2), (DOWN, 2), (FAR, 1))
    far(3)
    sums((UP, 3), (DOWN, 3), (FAR, 2), (FAR, 3))

    for copy in u_copies:
        copy.wait_send()
    pltpu.make_async_copy(given, given, give_send).wait()
    pltpu.make_async_copy(kbuf, kbuf, y_send).wait()
    pltpu.make_async_copy(xin, xin, x_send).wait()

    @pl.when(c == core_of_z)
    def _():
        sent = zbuf.at[pl.ds(1, Z - 1)]
        pltpu.make_async_copy(sent, sent, z_send).wait()

    @pl.when(c != core_of_z)
    def _():
        pltpu.make_async_copy(zbuf, zbuf, z_send).wait()

    @pl.when(c == core_of_z)
    def _():
        others = zbuf.at[pl.ds(1, Z - 1)]
        pltpu.make_async_copy(others, others, z_recv).wait()
        here = 32 * (z % 2) + 16 * c
        total = zsend[number_of_z, pl.ds(pl.multiple_of(here, 16), 16)].astype(jnp.float32)
        for d in range(1, Z):
            total = total + zbuf[d].astype(jnp.float32)
        out_ref[...] = total

    @pl.when(c != core_of_z)
    def _():
        pltpu.make_async_copy(zbuf, zbuf, z_recv).wait()
        total = zbuf[0].astype(jnp.float32)
        for d in range(1, Z):
            total = total + zbuf[d].astype(jnp.float32)
        out_ref[...] = total


def on_device(u_real, u_imag, psi_real, psi_imag, kick_angle, excited):
    rows, depth = u_real.shape
    bf16, f32 = jnp.bfloat16, jnp.float32
    any_place = pl.BlockSpec(memory_space=pl.ANY)
    vmem = pl.BlockSpec(memory_space=pltpu.VMEM)
    dma = pltpu.SemaphoreType.DMA
    out = pl.pallas_call(
        kernel,
        out_shape=pltpu.VMEM((16, rows), f32),
        in_specs=[any_place] * 6,
        out_specs=vmem,
        scratch_shapes=[
            pltpu.VMEM((1, 64), f32),
            pltpu.VMEM((1, depth), jnp.int32),
            pltpu.VMEM((2, 64, depth), bf16),
            pltpu.VMEM((C, 2, rows, depth), bf16),
            pltpu.VMEM((128, depth), bf16),
            pltpu.VMEM((128, 128), bf16),
            pltpu.VMEM((PIECES, 2 * PIECE, depth), bf16),
            pltpu.VMEM((2, 2 * PIECE, depth), bf16),
            pltpu.VMEM((PIECES, 3, 2 * PIECE, depth), bf16),
            pltpu.VMEM((Y, PIECES, 64, rows), bf16),
            pltpu.VMEM((PIECES, X - 1, 64, rows), bf16),
            pltpu.VMEM((PIECES, 64, rows), bf16),
            pltpu.VMEM((Z, 16, rows), bf16),
            dma((4,)),
            dma((2,)),
            dma((2,)),
            dma((2,)),
            dma,
            dma((PIECES,)),
            dma,
            dma((Y, PIECES)),
            dma,
            dma((PIECES,)),
            dma,
            dma,
            pltpu.SemaphoreType.REGULAR((6,)),
        ],
        compiler_params=pltpu.CompilerParams(
            collective_id=0, has_side_effects=True, vmem_limit_bytes=56 << 20
        ),
        cost_estimate=pl.CostEstimate(
            flops=4 * 2 * 256 * 256 * depth, bytes_accessed=6 * rows * depth * 2, transcendentals=0
        ),
    )(kick_angle[None, :], excited[None, :], psi_real.T, psi_imag.T, u_real, u_imag)
    return out[:8], out[8:]


def solution(mesh):
    split = Mesh(mesh.devices.reshape(Y, C, X, Z), ("y", "c", "x", "z"))
    return jax.shard_map(
        on_device,
        mesh=split,
        in_specs=(
            P(NARROW, WIDE),
            P(NARROW, WIDE),
            P(WIDE, NARROW),
            P(WIDE, NARROW),
            P(NARROW),
            P(WIDE),
        ),
        out_specs=(P(WIDE, NARROW), P(WIDE, NARROW)),
        check_vma=False,
    )
```

```python
import jax
import jax.numpy as jnp
from jax import lax
from jax.experimental import pallas as pl
from jax.experimental.pallas import tpu as pltpu
from jax.sharding import Mesh
from jax.sharding import PartitionSpec as P

Y, C, X, Z = 4, 2, 4, 16
NARROW = ("y", "c")
WIDE = ("x", "z")
PIECE = 16
PIECES = 4
MESH = pl.DeviceIdType.MESH

OWN, UP, FAR, DOWN = 0, 1, 2, 3
PLACE = {FAR: 0, UP: 1, DOWN: 2}
EARLY = 4
RELAY, Y_KNOWN, X_KNOWN, Z_KNOWN = range(4)
PAIRS = ((0, 2, 7, 5), (1, 3, 6, 4))
CORE_OF = tuple(0 if k in PAIRS[0] else 1 for k in range(Z // 2))
NUMBER_OF = tuple(PAIRS[CORE_OF[k]].index(k) for k in range(Z // 2))
KEPT = tuple([(k % 4, p) for p, k in enumerate(PAIRS[c]) if k // 4 == c] for c in range(C))
GIVEN = tuple([(k % 4, p) for p, k in enumerate(PAIRS[1 - c]) if k // 4 == c] for c in range(C))


def kernel(
    angle_hbm,
    excited_hbm,
    psi_real_hbm,
    psi_imag_hbm,
    u_real_hbm,
    u_imag_hbm,
    out_ref,
    angle,
    excited,
    psi,
    w,
    hot,
    table,
    own,
    given,
    kbuf,
    xsend,
    xin,
    zsend,
    zbuf,
    in_sem,
    u_sem,
    u_send,
    u_recv,
    give_send,
    give_recv,
    y_send,
    y_recv,
    x_send,
    x_recv,
    z_send,
    z_recv,
    known,
):
    y, c, x, z = (lax.axis_index(a) for a in ("y", "c", "x", "z"))
    up, down = lax.rem(y + 1, Y), lax.rem(y + Y - 1, Y)
    pair_of_z = z // 2
    core_of_z = sum(jnp.where(pair_of_z == k, CORE_OF[k], 0) for k in range(Z // 2))
    number_of_z = sum(jnp.where(pair_of_z == k, NUMBER_OF[k], 0) for k in range(Z // 2))

    def by_core(values):
        return jnp.where(c == 0, values[0], values[1])

    mine = lax.rem(x - y + Y, Y)
    depth = psi.shape[-1]

    barrier = pltpu.get_barrier_semaphore()

    def greet(**where):
        pl.semaphore_signal(barrier, inc=1, device_id=where, device_id_type=MESH)

    greet(y=up, c=0)
    greet(y=down, c=0)

    @pl.when(c == 1)
    def _():
        greet(c=0)

    for d in (1, X - 1):
        greet(x=lax.rem(x + d, X), c=0)


    loads = [
        pltpu.make_async_copy(angle_hbm, angle, in_sem.at[0]),
        pltpu.make_async_copy(excited_hbm, excited, in_sem.at[1]),
        pltpu.make_async_copy(psi_real_hbm, psi.at[0], in_sem.at[2]),
        pltpu.make_async_copy(psi_imag_hbm, psi.at[1], in_sem.at[3]),
        pltpu.make_async_copy(u_real_hbm, w.at[c, 0], u_sem.at[0]),
        pltpu.make_async_copy(u_imag_hbm, w.at[c, 1], u_sem.at[1]),
    ]
    for load in loads:
        load.start()

    def tell(what, **where):
        pl.semaphore_signal(known.at[what], inc=1, device_id=where, device_id_type=MESH)

    loads[0].wait()
    number = lax.broadcasted_iota(jnp.int32, (PIECE, 64), 0).astype(jnp.float32)
    phases = number * angle[...]
    full = jnp.concatenate([jnp.cos(phases), jnp.sin(phases)], axis=1)
    high = full.astype(jnp.bfloat16).astype(jnp.float32)
    rest = full - high
    middle = rest.astype(jnp.bfloat16).astype(jnp.float32)
    low = rest - middle
    terms = jnp.concatenate([high, middle, low, jnp.zeros((128 - 3 * PIECE, 128), jnp.float32)], axis=0)
    table[...] = terms.T.astype(jnp.bfloat16)
    loads[1].wait()
    row = lax.broadcasted_iota(jnp.int32, (128, depth), 0) % PIECE
    hot[...] = jnp.where(row == excited[...], 1.0, 0.0).astype(jnp.bfloat16)
    loads[2].wait()
    loads[3].wait()

    def kick(place, to):
        at = pl.ds(pl.multiple_of(PIECE * place, PIECE), PIECE)
        sines_at = pl.ds(pl.multiple_of(64 + PIECE * place, PIECE), PIECE)
        angles = jnp.concatenate([table[at, :], table[sines_at, :]], axis=0)
        turn = jnp.dot(angles, hot[...], preferred_element_type=jnp.float32)
        cosine, sine = turn[:PIECE], turn[PIECE:]
        real = psi[0, at, :].astype(jnp.float32)
        imag = psi[1, at, :].astype(jnp.float32)
        to[:PIECE] = (cosine * real + sine * imag).astype(jnp.bfloat16)
        to[PIECE:] = (cosine * imag - sine * real).astype(jnp.bfloat16)

    def keep(i):
        kick(by_core([KEPT[k][i][0] for k in range(C)]), own.at[by_core([KEPT[k][i][1] for k in range(C)])])

    def give(i):
        kick(by_core([GIVEN[k][i][0] for k in range(C)]), given.at[i])
        number = by_core([GIVEN[k][i][1] for k in range(C)])
        pltpu.make_async_remote_copy(
            src_ref=given.at[i],
            dst_ref=own.at[number],
            send_sem=give_send,
            recv_sem=give_recv.at[number],
            device_id={"c": 1 - c},
            device_id_type=MESH,
        ).start()

    def was_given(j):
        for k in range(C):
            if j in [p for _, p in GIVEN[1 - k]]:

                @pl.when(c == k)
                def _():
                    pltpu.make_async_copy(own.at[j], own.at[j], give_recv.at[j]).wait()

    def own_to(j, slot, where):
        return pltpu.make_async_remote_copy(
            src_ref=own.at[j],
            dst_ref=kbuf.at[j, PLACE[slot]],
            send_sem=y_send,
            recv_sem=y_recv.at[slot, j],
            device_id={"y": where},
            device_id_type=MESH,
        )

    def send_own(j):
        own_to(j, DOWN, up).start()
        own_to(j, UP, down).start()

    def pass_on(slot, j):
        part = pl.ds(0, PIECE) if slot == DOWN else pl.ds(PIECE, PIECE)
        pltpu.make_async_remote_copy(
            src_ref=kbuf.at[j, PLACE[slot], part],
            dst_ref=kbuf.at[j, PLACE[FAR], part],
            send_sem=y_send,
            recv_sem=y_recv.at[FAR, j],
            device_id={"y": up if slot == DOWN else down},
            device_id_type=MESH,
        ).start()

    def arrived(slot, j):
        own_to(j, slot, up).wait_recv()

    def pair_arrived(j):
        arrived(DOWN, j)
        pass_on(DOWN, j)
        arrived(UP, j)
        pass_on(UP, j)

    keep(0)

    @pl.when(c == 0)
    def _():
        pl.semaphore_wait(barrier, 9)
        tell(Y_KNOWN, c=1)
        send_own(0)
        for d in (1, X - 1):
            tell(RELAY, x=lax.rem(x + d, X))

    @pl.when(c == 1)
    def _():
        pl.semaphore_wait(known.at[Y_KNOWN], 1)

    u_copies = [
        pltpu.make_async_remote_copy(
            src_ref=u,
            dst_ref=w.at[c, i],
            send_sem=u_send.at[i],
            recv_sem=u_recv.at[i],
            device_id={"c": 1 - c},
            device_id_type=MESH,
        )
        for i, u in enumerate((u_real_hbm, u_imag_hbm))
    ]
    @pl.loop(1, Z)
    def _(d):
        greet(z=lax.rem(z + d, Z), c=1)

    give(0)
    give(1)
    for copy in u_copies:
        copy.start()
    keep(1)

    @pl.when(c == 0)
    def _():
        send_own(1)

    was_given(0)
    pl.when(c == 1)(lambda: send_own(0))
    was_given(1)
    pl.when(c == 1)(lambda: send_own(1))
    was_given(2)
    pair_arrived(0)
    send_own(2)
    was_given(3)

    loads[4].wait()
    loads[5].wait()
    for i, u in enumerate((u_real_hbm, u_imag_hbm)):
        pltpu.make_async_remote_copy(
            src_ref=u,
            dst_ref=w.at[1 - c, i],
            send_sem=u_send.at[i],
            recv_sem=u_recv.at[i],
            device_id={"c": 1 - c},
            device_id_type=MESH,
        ).wait_recv()

    def multiply(states, pieces):
        products = lax.dot_general(
            states,
            w[...].reshape(4 * 128, depth),
            (((1,), (1,)), ((), ())),
            preferred_element_type=jnp.float32,
        )
        for i, (slot, j) in enumerate(pieces):
            by_real = products[2 * PIECE * i : 2 * PIECE * i + PIECE]
            by_imag = products[2 * PIECE * i + PIECE : 2 * PIECE * (i + 1)]
            parts = []
            for r in range(C):
                at_real, at_imag = slice(256 * r, 256 * r + 128), slice(256 * r + 128, 256 * (r + 1))
                parts.append(by_real[:, at_real] - by_imag[:, at_imag])
                parts.append(by_imag[:, at_real] + by_real[:, at_imag])
            xsend[slot, j] = jnp.concatenate(
                [part[8 * h : 8 * (h + 1)] for h in range(2) for part in parts], axis=0
            ).astype(jnp.bfloat16)

            @pl.when(slot != mine)
            def _():
                owner = lax.rem(y + slot, Y)
                pltpu.make_async_remote_copy(
                    src_ref=xsend.at[slot, j],
                    dst_ref=xin.at[j, lax.rem(x - owner + X, X) - 1],
                    send_sem=x_send,
                    recv_sem=x_recv.at[j],
                    device_id={"x": owner},
                    device_id_type=MESH,
                ).start()

    def sum_over_x(slot, j):
        @pl.when(slot == mine)
        def _():
            pltpu.make_async_copy(xin.at[j], xin.at[j], x_recv.at[j]).wait()
            total = xsend[slot, j].astype(jnp.float32)
            for d in range(X - 1):
                total = total + xin[j, d].astype(jnp.float32)
            zsend[j] = total.astype(jnp.bfloat16)
            for h in range(2):
                target = 2 * by_core([PAIRS[k][j] for k in range(C)]) + h
                for r in range(C):

                    @pl.when(jnp.logical_or(target != z, c != r))
                    def _():
                        pltpu.make_async_remote_copy(
                            src_ref=zsend.at[j, pl.ds(32 * h + 16 * r, 16)],
                            dst_ref=zbuf.at[lax.rem(z - target + Z, Z)],
                            send_sem=z_send,
                            recv_sem=z_recv,
                            device_id={"z": target, "c": r},
                            device_id_type=MESH,
                        ).start()

    def pair(j):
        multiply(kbuf[j, 1:3].reshape(4 * PIECE, depth), [(UP, j), (DOWN, j)])

    def far(j):
        arrived(FAR, j)
        multiply(kbuf[j, 0], [(FAR, j)])

    @pl.when(c == 0)
    def _():
        pl.semaphore_wait(known.at[RELAY], 2)
        tell(X_KNOWN, c=1)

    @pl.when(c == 1)
    def _():
        pl.semaphore_wait(known.at[X_KNOWN], 1)

    multiply(own[...].reshape(8 * PIECE, depth), [(OWN, j) for j in range(PIECES)])

    pair(0)

    def know_z():
        @pl.when(c == 1)
        def _():
            pl.semaphore_wait(barrier, 2 * (Z - 1))
            tell(Z_KNOWN, c=0)

        @pl.when(c == 0)
        def _():
            pl.semaphore_wait(known.at[Z_KNOWN], 1)

    def sums(*which):
        for slot, j in which:
            sum_over_x(slot, j)

    early = z < EARLY

    def first_sums():
        sums((OWN, 0), (UP, 0), (DOWN, 0))

    def second_sums():
        sums((FAR, 0))

    def third_sums():
        sums((OWN, 1), (UP, 1), (DOWN, 1), (OWN, 2), (OWN, 3))

    pair_arrived(1)
    send_own(3)
    far(0)
    pair(1)

    @pl.when(jnp.logical_not(early))
    def _():
        know_z()
        first_sums()

    pair_arrived(2)

    @pl.when(jnp.logical_not(early))
    def _():
        second_sums()

    pair(2)
    far(1)
    pair_arrived(3)

    @pl.when(jnp.logical_not(early))
    def _():
        third_sums()

    pair(3)

    @pl.when(early)
    def _():
        know_z()
        first_sums()
        second_sums()
        third_sums()

    far(2)
    sums((UP, 2), (DOWN, 2), (FAR, 1))
    far(3)
    sums((UP, 3), (DOWN, 3), (FAR, 2), (FAR, 3))

    for copy in u_copies:
        copy.wait_send()
    pltpu.make_async_copy(given, given, give_send).wait()
    pltpu.make_async_copy(kbuf, kbuf, y_send).wait()
    pltpu.make_async_copy(xin, xin, x_send).wait()

    @pl.when(c == core_of_z)
    def _():
        sent = zbuf.at[pl.ds(1, Z - 1)]
        pltpu.make_async_copy(sent, sent, z_send).wait()

    @pl.when(c != core_of_z)
    def _():
        pltpu.make_async_copy(zbuf, zbuf, z_send).wait()

    @pl.when(c == core_of_z)
    def _():
        others = zbuf.at[pl.ds(1, Z - 1)]
        pltpu.make_async_copy(others, others, z_recv).wait()
        here = 32 * (z % 2) + 16 * c
        total = zsend[number_of_z, pl.ds(pl.multiple_of(here, 16), 16)].astype(jnp.float32)
        for d in range(1, Z):
            total = total + zbuf[d].astype(jnp.float32)
        out_ref[...] = total

    @pl.when(c != core_of_z)
    def _():
        pltpu.make_async_copy(zbuf, zbuf, z_recv).wait()
        total = zbuf[0].astype(jnp.float32)
        for d in range(1, Z):
            total = total + zbuf[d].astype(jnp.float32)
        out_ref[...] = total


def on_device(u_real, u_imag, psi_real, psi_imag, kick_angle, excited):
    rows, depth = u_real.shape
    bf16, f32 = jnp.bfloat16, jnp.float32
    any_place = pl.BlockSpec(memory_space=pl.ANY)
    vmem = pl.BlockSpec(memory_space=pltpu.VMEM)
    dma = pltpu.SemaphoreType.DMA
    out = pl.pallas_call(
        kernel,
        out_shape=pltpu.VMEM((16, rows), f32),
        in_specs=[any_place] * 6,
        out_specs=vmem,
        scratch_shapes=[
            pltpu.VMEM((1, 64), f32),
            pltpu.VMEM((1, depth), jnp.int32),
            pltpu.VMEM((2, 64, depth), bf16),
            pltpu.VMEM((C, 2, rows, depth), bf16),
            pltpu.VMEM((128, depth), bf16),
            pltpu.VMEM((128, 128), bf16),
            pltpu.VMEM((PIECES, 2 * PIECE, depth), bf16),
            pltpu.VMEM((2, 2 * PIECE, depth), bf16),
            pltpu.VMEM((PIECES, 3, 2 * PIECE, depth), bf16),
            pltpu.VMEM((Y, PIECES, 64, rows), bf16),
            pltpu.VMEM((PIECES, X - 1, 64, rows), bf16),
            pltpu.VMEM((PIECES, 64, rows), bf16),
            pltpu.VMEM((Z, 16, rows), bf16),
            dma((4,)),
            dma((2,)),
            dma((2,)),
            dma((2,)),
            dma,
            dma((PIECES,)),
            dma,
            dma((Y, PIECES)),
            dma,
            dma((PIECES,)),
            dma,
            dma,
            pltpu.SemaphoreType.REGULAR((4,)),
        ],
        compiler_params=pltpu.CompilerParams(
            collective_id=0, has_side_effects=True, vmem_limit_bytes=56 << 20
        ),
        cost_estimate=pl.CostEstimate(
            flops=4 * 2 * 256 * 256 * depth, bytes_accessed=6 * rows * depth * 2, transcendentals=0
        ),
    )(kick_angle[None, :], excited[None, :], psi_real.T, psi_imag.T, u_real, u_imag)
    return out[:8], out[8:]


def solution(mesh):
    split = Mesh(mesh.devices.reshape(Y, C, X, Z), ("y", "c", "x", "z"))
    return jax.shard_map(
        on_device,
        mesh=split,
        in_specs=(
            P(NARROW, WIDE),
            P(NARROW, WIDE),
            P(WIDE, NARROW),
            P(WIDE, NARROW),
            P(NARROW),
            P(WIDE),
        ),
        out_specs=(P(WIDE, NARROW), P(WIDE, NARROW)),
        check_vma=False,
    )
```

```python
import jax
import jax.numpy as jnp
from jax import lax
from jax.experimental import pallas as pl
from jax.experimental.pallas import tpu as pltpu
from jax.sharding import Mesh
from jax.sharding import PartitionSpec as P

Y, C, X, Z = 4, 2, 4, 16
NARROW = ("y", "c")
WIDE = ("x", "z")
PIECE = 16
PIECES = 4
MESH = pl.DeviceIdType.MESH

OWN, UP, FAR, DOWN = 0, 1, 2, 3
PLACE = {FAR: 0, UP: 1, DOWN: 2}
EARLY = 4
RELAY, Y_KNOWN, X_KNOWN, Z_KNOWN = range(4)
PAIRS = ((0, 2, 7, 5), (1, 3, 6, 4))
CORE_OF = tuple(0 if k in PAIRS[0] else 1 for k in range(Z // 2))
NUMBER_OF = tuple(PAIRS[CORE_OF[k]].index(k) for k in range(Z // 2))
KEPT = tuple([(k % 4, p) for p, k in enumerate(PAIRS[c]) if k // 4 == c] for c in range(C))
GIVEN = tuple([(k % 4, p) for p, k in enumerate(PAIRS[1 - c]) if k // 4 == c] for c in range(C))


def kernel(
    angle_hbm,
    excited_hbm,
    psi_real_hbm,
    psi_imag_hbm,
    u_real_hbm,
    u_imag_hbm,
    out_ref,
    angle,
    excited,
    psi,
    w,
    hot,
    table,
    own,
    given,
    kbuf,
    xsend,
    xin,
    zsend,
    zbuf,
    in_sem,
    u_sem,
    u_send,
    u_recv,
    give_send,
    give_recv,
    y_send,
    y_recv,
    x_send,
    x_recv,
    z_send,
    z_recv,
    known,
):
    y, c, x, z = (lax.axis_index(a) for a in ("y", "c", "x", "z"))
    up, down = lax.rem(y + 1, Y), lax.rem(y + Y - 1, Y)
    pair_of_z = z // 2
    core_of_z = sum(jnp.where(pair_of_z == k, CORE_OF[k], 0) for k in range(Z // 2))
    number_of_z = sum(jnp.where(pair_of_z == k, NUMBER_OF[k], 0) for k in range(Z // 2))

    def by_core(values):
        return jnp.where(c == 0, values[0], values[1])

    mine = lax.rem(x - y + Y, Y)
    depth = psi.shape[-1]

    barrier = pltpu.get_barrier_semaphore()

    def greet(**where):
        pl.semaphore_signal(barrier, inc=1, device_id=where, device_id_type=MESH)

    greet(y=up, c=0)
    greet(y=down, c=0)

    @pl.when(c == 1)
    def _():
        greet(c=0)

    for d in (1, X - 1):
        greet(x=lax.rem(x + d, X), c=0)


    loads = [
        pltpu.make_async_copy(angle_hbm, angle, in_sem.at[0]),
        pltpu.make_async_copy(excited_hbm, excited, in_sem.at[1]),
        pltpu.make_async_copy(psi_real_hbm, psi.at[0], in_sem.at[2]),
        pltpu.make_async_copy(psi_imag_hbm, psi.at[1], in_sem.at[3]),
        pltpu.make_async_copy(u_real_hbm, w.at[c, 0], u_sem.at[0]),
        pltpu.make_async_copy(u_imag_hbm, w.at[c, 1], u_sem.at[1]),
    ]
    for load in loads:
        load.start()

    def tell(what, **where):
        pl.semaphore_signal(known.at[what], inc=1, device_id=where, device_id_type=MESH)

    loads[0].wait()
    number = lax.broadcasted_iota(jnp.int32, (PIECE, 64), 0).astype(jnp.float32)
    phases = number * angle[...]
    full = jnp.concatenate([jnp.cos(phases), jnp.sin(phases)], axis=1)
    high = full.astype(jnp.bfloat16).astype(jnp.float32)
    rest = full - high
    middle = rest.astype(jnp.bfloat16).astype(jnp.float32)
    low = rest - middle
    terms = jnp.concatenate([high, middle, low, jnp.zeros((128 - 3 * PIECE, 128), jnp.float32)], axis=0)
    table[...] = terms.T.astype(jnp.bfloat16)
    loads[1].wait()
    row = lax.broadcasted_iota(jnp.int32, (128, depth), 0) % PIECE
    hot[...] = jnp.where(row == excited[...], 1.0, 0.0).astype(jnp.bfloat16)
    loads[2].wait()
    loads[3].wait()

    def kick(place, to):
        at = pl.ds(pl.multiple_of(PIECE * place, PIECE), PIECE)
        sines_at = pl.ds(pl.multiple_of(64 + PIECE * place, PIECE), PIECE)
        angles = jnp.concatenate([table[at, :], table[sines_at, :]], axis=0)
        turn = jnp.dot(angles, hot[...], preferred_element_type=jnp.float32)
        cosine, sine = turn[:PIECE], turn[PIECE:]
        real = psi[0, at, :].astype(jnp.float32)
        imag = psi[1, at, :].astype(jnp.float32)
        to[:PIECE] = (cosine * real + sine * imag).astype(jnp.bfloat16)
        to[PIECE:] = (cosine * imag - sine * real).astype(jnp.bfloat16)

    def keep(i):
        kick(by_core([KEPT[k][i][0] for k in range(C)]), own.at[by_core([KEPT[k][i][1] for k in range(C)])])

    def give(i):
        kick(by_core([GIVEN[k][i][0] for k in range(C)]), given.at[i])
        number = by_core([GIVEN[k][i][1] for k in range(C)])
        pltpu.make_async_remote_copy(
            src_ref=given.at[i],
            dst_ref=own.at[number],
            send_sem=give_send,
            recv_sem=give_recv.at[number],
            device_id={"c": 1 - c},
            device_id_type=MESH,
        ).start()

    def was_given(j):
        for k in range(C):
            if j in [p for _, p in GIVEN[1 - k]]:

                @pl.when(c == k)
                def _():
                    pltpu.make_async_copy(own.at[j], own.at[j], give_recv.at[j]).wait()

    def own_to(j, slot, where):
        return pltpu.make_async_remote_copy(
            src_ref=own.at[j],
            dst_ref=kbuf.at[j, PLACE[slot]],
            send_sem=y_send,
            recv_sem=y_recv.at[slot, j],
            device_id={"y": where},
            device_id_type=MESH,
        )

    def send_own(j):
        own_to(j, DOWN, up).start()
        own_to(j, UP, down).start()

    def pass_on(slot, j):
        part = pl.ds(0, PIECE) if slot == DOWN else pl.ds(PIECE, PIECE)
        pltpu.make_async_remote_copy(
            src_ref=kbuf.at[j, PLACE[slot], part],
            dst_ref=kbuf.at[j, PLACE[FAR], part],
            send_sem=y_send,
            recv_sem=y_recv.at[FAR, j],
            device_id={"y": up if slot == DOWN else down},
            device_id_type=MESH,
        ).start()

    def arrived(slot, j):
        own_to(j, slot, up).wait_recv()

    def pair_arrived(j):
        arrived(DOWN, j)
        pass_on(DOWN, j)
        arrived(UP, j)
        pass_on(UP, j)

    keep(0)

    @pl.when(c == 0)
    def _():
        pl.semaphore_wait(barrier, 9)
        tell(Y_KNOWN, c=1)
        send_own(0)
        for d in (1, X - 1):
            tell(RELAY, x=lax.rem(x + d, X))

    @pl.when(c == 1)
    def _():
        pl.semaphore_wait(known.at[Y_KNOWN], 1)

    u_copies = [
        pltpu.make_async_remote_copy(
            src_ref=u,
            dst_ref=w.at[c, i],
            send_sem=u_send.at[i],
            recv_sem=u_recv.at[i],
            device_id={"c": 1 - c},
            device_id_type=MESH,
        )
        for i, u in enumerate((u_real_hbm, u_imag_hbm))
    ]
    @pl.loop(1, Z)
    def _(d):
        greet(z=lax.rem(z + d, Z), c=1)

    give(0)
    give(1)
    for copy in u_copies:
        copy.start()
    keep(1)

    @pl.when(c == 0)
    def _():
        send_own(1)

    was_given(0)
    pl.when(c == 1)(lambda: send_own(0))
    was_given(1)
    pl.when(c == 1)(lambda: send_own(1))
    was_given(2)
    pair_arrived(0)
    send_own(2)
    was_given(3)

    loads[4].wait()
    loads[5].wait()
    for i, u in enumerate((u_real_hbm, u_imag_hbm)):
        pltpu.make_async_remote_copy(
            src_ref=u,
            dst_ref=w.at[1 - c, i],
            send_sem=u_send.at[i],
            recv_sem=u_recv.at[i],
            device_id={"c": 1 - c},
            device_id_type=MESH,
        ).wait_recv()

    def multiply(states, pieces):
        products = lax.dot_general(
            states,
            w[...].reshape(4 * 128, depth),
            (((1,), (1,)), ((), ())),
            preferred_element_type=jnp.float32,
        )
        for i, (slot, j) in enumerate(pieces):
            by_real = products[2 * PIECE * i : 2 * PIECE * i + PIECE]
            by_imag = products[2 * PIECE * i + PIECE : 2 * PIECE * (i + 1)]
            parts = []
            for r in range(C):
                at_real, at_imag = slice(256 * r, 256 * r + 128), slice(256 * r + 128, 256 * (r + 1))
                parts.append(by_real[:, at_real] - by_imag[:, at_imag])
                parts.append(by_imag[:, at_real] + by_real[:, at_imag])
            xsend[slot, j] = jnp.concatenate(
                [part[8 * h : 8 * (h + 1)] for h in range(2) for part in parts], axis=0
            ).astype(jnp.bfloat16)

            @pl.when(slot != mine)
            def _():
                owner = lax.rem(y + slot, Y)
                pltpu.make_async_remote_copy(
                    src_ref=xsend.at[slot, j],
                    dst_ref=xin.at[j, lax.rem(x - owner + X, X) - 1],
                    send_sem=x_send,
                    recv_sem=x_recv.at[j],
                    device_id={"x": owner},
                    device_id_type=MESH,
                ).start()

    def sum_over_x(slot, j):
        @pl.when(slot == mine)
        def _():
            pltpu.make_async_copy(xin.at[j], xin.at[j], x_recv.at[j]).wait()
            total = xsend[slot, j].astype(jnp.float32)
            for d in range(X - 1):
                total = total + xin[j, d].astype(jnp.float32)
            zsend[j] = total.astype(jnp.bfloat16)
            for h in range(2):
                target = 2 * by_core([PAIRS[k][j] for k in range(C)]) + h
                for r in range(C):

                    @pl.when(jnp.logical_or(target != z, c != r))
                    def _():
                        pltpu.make_async_remote_copy(
                            src_ref=zsend.at[j, pl.ds(32 * h + 16 * r, 16)],
                            dst_ref=zbuf.at[lax.rem(z - target + Z, Z)],
                            send_sem=z_send,
                            recv_sem=z_recv,
                            device_id={"z": target, "c": r},
                            device_id_type=MESH,
                        ).start()

    def pair(j):
        multiply(kbuf[j, 1:3].reshape(4 * PIECE, depth), [(UP, j), (DOWN, j)])

    def far(j):
        arrived(FAR, j)
        multiply(kbuf[j, 0], [(FAR, j)])

    @pl.when(c == 0)
    def _():
        pl.semaphore_wait(known.at[RELAY], 2)
        tell(X_KNOWN, c=1)

    @pl.when(c == 1)
    def _():
        pl.semaphore_wait(known.at[X_KNOWN], 1)

    multiply(own[...].reshape(8 * PIECE, depth), [(OWN, j) for j in range(PIECES)])

    pair(0)

    def hear_z():
        pl.semaphore_wait(barrier, 2 * (Z - 1))
        tell(Z_KNOWN, c=0)

    pl.when(jnp.logical_and(c == 1, z >= 8))(hear_z)

    def know_z():
        @pl.when(jnp.logical_and(c == 1, z < 8))
        def _():
            hear_z()

        @pl.when(c == 0)
        def _():
            pl.semaphore_wait(known.at[Z_KNOWN], 1)

    def sums(*which):
        for slot, j in which:
            sum_over_x(slot, j)

    early = z < EARLY

    def first_sums():
        sums((OWN, 0), (UP, 0), (DOWN, 0))

    def second_sums():
        sums((FAR, 0))

    def third_sums():
        sums((OWN, 1), (UP, 1), (DOWN, 1), (OWN, 2), (OWN, 3))

    pair_arrived(1)
    send_own(3)
    far(0)
    pair(1)

    @pl.when(jnp.logical_not(early))
    def _():
        know_z()
        first_sums()

    pair_arrived(2)

    @pl.when(jnp.logical_not(early))
    def _():
        second_sums()

    pair(2)
    far(1)
    pair_arrived(3)

    @pl.when(jnp.logical_not(early))
    def _():
        third_sums()

    pair(3)

    @pl.when(early)
    def _():
        know_z()
        first_sums()
        second_sums()
        third_sums()

    far(2)
    sums((UP, 2), (DOWN, 2), (FAR, 1))
    far(3)
    sums((UP, 3), (DOWN, 3), (FAR, 2), (FAR, 3))

    for copy in u_copies:
        copy.wait_send()
    pltpu.make_async_copy(given, given, give_send).wait()
    pltpu.make_async_copy(kbuf, kbuf, y_send).wait()
    pltpu.make_async_copy(xin, xin, x_send).wait()

    @pl.when(c == core_of_z)
    def _():
        sent = zbuf.at[pl.ds(1, Z - 1)]
        pltpu.make_async_copy(sent, sent, z_send).wait()

    @pl.when(c != core_of_z)
    def _():
        pltpu.make_async_copy(zbuf, zbuf, z_send).wait()

    @pl.when(c == core_of_z)
    def _():
        others = zbuf.at[pl.ds(1, Z - 1)]
        pltpu.make_async_copy(others, others, z_recv).wait()
        here = 32 * (z % 2) + 16 * c
        total = zsend[number_of_z, pl.ds(pl.multiple_of(here, 16), 16)].astype(jnp.float32)
        for d in range(1, Z):
            total = total + zbuf[d].astype(jnp.float32)
        out_ref[...] = total

    @pl.when(c != core_of_z)
    def _():
        pltpu.make_async_copy(zbuf, zbuf, z_recv).wait()
        total = zbuf[0].astype(jnp.float32)
        for d in range(1, Z):
            total = total + zbuf[d].astype(jnp.float32)
        out_ref[...] = total


def on_device(u_real, u_imag, psi_real, psi_imag, kick_angle, excited):
    rows, depth = u_real.shape
    bf16, f32 = jnp.bfloat16, jnp.float32
    any_place = pl.BlockSpec(memory_space=pl.ANY)
    vmem = pl.BlockSpec(memory_space=pltpu.VMEM)
    dma = pltpu.SemaphoreType.DMA
    out = pl.pallas_call(
        kernel,
        out_shape=pltpu.VMEM((16, rows), f32),
        in_specs=[any_place] * 6,
        out_specs=vmem,
        scratch_shapes=[
            pltpu.VMEM((1, 64), f32),
            pltpu.VMEM((1, depth), jnp.int32),
            pltpu.VMEM((2, 64, depth), bf16),
            pltpu.VMEM((C, 2, rows, depth), bf16),
            pltpu.VMEM((128, depth), bf16),
            pltpu.VMEM((128, 128), bf16),
            pltpu.VMEM((PIECES, 2 * PIECE, depth), bf16),
            pltpu.VMEM((2, 2 * PIECE, depth), bf16),
            pltpu.VMEM((PIECES, 3, 2 * PIECE, depth), bf16),
            pltpu.VMEM((Y, PIECES, 64, rows), bf16),
            pltpu.VMEM((PIECES, X - 1, 64, rows), bf16),
            pltpu.VMEM((PIECES, 64, rows), bf16),
            pltpu.VMEM((Z, 16, rows), bf16),
            dma((4,)),
            dma((2,)),
            dma((2,)),
            dma((2,)),
            dma,
            dma((PIECES,)),
            dma,
            dma((Y, PIECES)),
            dma,
            dma((PIECES,)),
            dma,
            dma,
            pltpu.SemaphoreType.REGULAR((4,)),
        ],
        compiler_params=pltpu.CompilerParams(
            collective_id=0, has_side_effects=True, vmem_limit_bytes=56 << 20
        ),
        cost_estimate=pl.CostEstimate(
            flops=4 * 2 * 256 * 256 * depth, bytes_accessed=6 * rows * depth * 2, transcendentals=0
        ),
    )(kick_angle[None, :], excited[None, :], psi_real.T, psi_imag.T, u_real, u_imag)
    return out[:8], out[8:]


def solution(mesh):
    split = Mesh(mesh.devices.reshape(Y, C, X, Z), ("y", "c", "x", "z"))
    return jax.shard_map(
        on_device,
        mesh=split,
        in_specs=(
            P(NARROW, WIDE),
            P(NARROW, WIDE),
            P(WIDE, NARROW),
            P(WIDE, NARROW),
            P(NARROW),
            P(WIDE),
        ),
        out_specs=(P(WIDE, NARROW), P(WIDE, NARROW)),
        check_vma=False,
    )
```

```python
import jax
import jax.numpy as jnp
from jax import lax
from jax.experimental import pallas as pl
from jax.experimental.pallas import tpu as pltpu
from jax.sharding import Mesh
from jax.sharding import PartitionSpec as P

Y, C, X, Z = 4, 2, 4, 16
NARROW = ("y", "c")
WIDE = ("x", "z")
PIECE = 16
PIECES = 4
MESH = pl.DeviceIdType.MESH

OWN, UP, FAR, DOWN = 0, 1, 2, 3
PLACE = {FAR: 0, UP: 1, DOWN: 2}
EARLY = 4
RELAY, Y_KNOWN, X_KNOWN, Z_KNOWN = range(4)
PAIRS = ((0, 2, 6, 5), (1, 7, 3, 4))
CORE_OF = tuple(0 if k in PAIRS[0] else 1 for k in range(Z // 2))
NUMBER_OF = tuple(PAIRS[CORE_OF[k]].index(k) for k in range(Z // 2))
KEPT = tuple([(k % 4, p) for p, k in enumerate(PAIRS[c]) if k // 4 == c] for c in range(C))
GIVEN = tuple([(k % 4, p) for p, k in enumerate(PAIRS[1 - c]) if k // 4 == c] for c in range(C))


def kernel(
    angle_hbm,
    excited_hbm,
    psi_real_hbm,
    psi_imag_hbm,
    u_real_hbm,
    u_imag_hbm,
    out_ref,
    angle,
    excited,
    psi,
    w,
    hot,
    table,
    own,
    given,
    kbuf,
    xsend,
    xin,
    zsend,
    zbuf,
    in_sem,
    u_sem,
    u_send,
    u_recv,
    give_send,
    give_recv,
    y_send,
    y_recv,
    x_send,
    x_recv,
    z_send,
    z_recv,
    known,
):
    y, c, x, z = (lax.axis_index(a) for a in ("y", "c", "x", "z"))
    up, down = lax.rem(y + 1, Y), lax.rem(y + Y - 1, Y)
    pair_of_z = z // 2
    core_of_z = sum(jnp.where(pair_of_z == k, CORE_OF[k], 0) for k in range(Z // 2))
    number_of_z = sum(jnp.where(pair_of_z == k, NUMBER_OF[k], 0) for k in range(Z // 2))

    def by_core(values):
        return jnp.where(c == 0, values[0], values[1])

    mine = lax.rem(x - y + Y, Y)
    depth = psi.shape[-1]

    barrier = pltpu.get_barrier_semaphore()

    def greet(**where):
        pl.semaphore_signal(barrier, inc=1, device_id=where, device_id_type=MESH)

    greet(y=up, c=0)
    greet(y=down, c=0)

    @pl.when(c == 1)
    def _():
        greet(c=0)

    for d in (1, X - 1):
        greet(x=lax.rem(x + d, X), c=0)


    loads = [
        pltpu.make_async_copy(angle_hbm, angle, in_sem.at[0]),
        pltpu.make_async_copy(excited_hbm, excited, in_sem.at[1]),
        pltpu.make_async_copy(psi_real_hbm, psi.at[0], in_sem.at[2]),
        pltpu.make_async_copy(psi_imag_hbm, psi.at[1], in_sem.at[3]),
        pltpu.make_async_copy(u_real_hbm, w.at[c, 0], u_sem.at[0]),
        pltpu.make_async_copy(u_imag_hbm, w.at[c, 1], u_sem.at[1]),
    ]
    for load in loads:
        load.start()

    def tell(what, **where):
        pl.semaphore_signal(known.at[what], inc=1, device_id=where, device_id_type=MESH)

    loads[0].wait()
    number = lax.broadcasted_iota(jnp.int32, (PIECE, 64), 0).astype(jnp.float32)
    phases = number * angle[...]
    full = jnp.concatenate([jnp.cos(phases), jnp.sin(phases)], axis=1)
    high = full.astype(jnp.bfloat16).astype(jnp.float32)
    rest = full - high
    middle = rest.astype(jnp.bfloat16).astype(jnp.float32)
    low = rest - middle
    terms = jnp.concatenate([high, middle, low, jnp.zeros((128 - 3 * PIECE, 128), jnp.float32)], axis=0)
    table[...] = terms.T.astype(jnp.bfloat16)
    loads[1].wait()
    row = lax.broadcasted_iota(jnp.int32, (128, depth), 0) % PIECE
    hot[...] = jnp.where(row == excited[...], 1.0, 0.0).astype(jnp.bfloat16)
    loads[2].wait()
    loads[3].wait()

    def kick(place, to):
        at = pl.ds(pl.multiple_of(PIECE * place, PIECE), PIECE)
        sines_at = pl.ds(pl.multiple_of(64 + PIECE * place, PIECE), PIECE)
        angles = jnp.concatenate([table[at, :], table[sines_at, :]], axis=0)
        turn = jnp.dot(angles, hot[...], preferred_element_type=jnp.float32)
        cosine, sine = turn[:PIECE], turn[PIECE:]
        real = psi[0, at, :].astype(jnp.float32)
        imag = psi[1, at, :].astype(jnp.float32)
        to[:PIECE] = (cosine * real + sine * imag).astype(jnp.bfloat16)
        to[PIECE:] = (cosine * imag - sine * real).astype(jnp.bfloat16)

    def keep(i):
        kick(by_core([KEPT[k][i][0] for k in range(C)]), own.at[by_core([KEPT[k][i][1] for k in range(C)])])

    def give(i):
        kick(by_core([GIVEN[k][i][0] for k in range(C)]), given.at[i])
        number = by_core([GIVEN[k][i][1] for k in range(C)])
        pltpu.make_async_remote_copy(
            src_ref=given.at[i],
            dst_ref=own.at[number],
            send_sem=give_send,
            recv_sem=give_recv.at[number],
            device_id={"c": 1 - c},
            device_id_type=MESH,
        ).start()

    def was_given(j):
        for k in range(C):
            if j in [p for _, p in GIVEN[1 - k]]:

                @pl.when(c == k)
                def _():
                    pltpu.make_async_copy(own.at[j], own.at[j], give_recv.at[j]).wait()

    def own_to(j, slot, where):
        return pltpu.make_async_remote_copy(
            src_ref=own.at[j],
            dst_ref=kbuf.at[j, PLACE[slot]],
            send_sem=y_send,
            recv_sem=y_recv.at[slot, j],
            device_id={"y": where},
            device_id_type=MESH,
        )

    def send_own(j):
        own_to(j, DOWN, up).start()
        own_to(j, UP, down).start()

    def pass_on(slot, j):
        part = pl.ds(0, PIECE) if slot == DOWN else pl.ds(PIECE, PIECE)
        pltpu.make_async_remote_copy(
            src_ref=kbuf.at[j, PLACE[slot], part],
            dst_ref=kbuf.at[j, PLACE[FAR], part],
            send_sem=y_send,
            recv_sem=y_recv.at[FAR, j],
            device_id={"y": up if slot == DOWN else down},
            device_id_type=MESH,
        ).start()

    def arrived(slot, j):
        own_to(j, slot, up).wait_recv()

    def pair_arrived(j):
        arrived(DOWN, j)
        pass_on(DOWN, j)
        arrived(UP, j)
        pass_on(UP, j)

    keep(0)

    @pl.when(c == 0)
    def _():
        pl.semaphore_wait(barrier, 9)
        tell(Y_KNOWN, c=1)
        send_own(0)
        for d in (1, X - 1):
            tell(RELAY, x=lax.rem(x + d, X))

    @pl.when(c == 1)
    def _():
        pl.semaphore_wait(known.at[Y_KNOWN], 1)

    u_copies = [
        pltpu.make_async_remote_copy(
            src_ref=u,
            dst_ref=w.at[c, i],
            send_sem=u_send.at[i],
            recv_sem=u_recv.at[i],
            device_id={"c": 1 - c},
            device_id_type=MESH,
        )
        for i, u in enumerate((u_real_hbm, u_imag_hbm))
    ]
    @pl.loop(1, Z)
    def _(d):
        greet(z=lax.rem(z + d, Z), c=1)

    give(0)
    give(1)
    for copy in u_copies:
        copy.start()
    keep(1)

    @pl.when(c == 0)
    def _():
        send_own(1)

    was_given(0)
    pl.when(c == 1)(lambda: send_own(0))
    was_given(1)
    pl.when(c == 1)(lambda: send_own(1))
    was_given(2)
    pair_arrived(0)
    send_own(2)
    was_given(3)

    loads[4].wait()
    loads[5].wait()
    for i, u in enumerate((u_real_hbm, u_imag_hbm)):
        pltpu.make_async_remote_copy(
            src_ref=u,
            dst_ref=w.at[1 - c, i],
            send_sem=u_send.at[i],
            recv_sem=u_recv.at[i],
            device_id={"c": 1 - c},
            device_id_type=MESH,
        ).wait_recv()

    def multiply(states, pieces):
        products = lax.dot_general(
            states,
            w[...].reshape(4 * 128, depth),
            (((1,), (1,)), ((), ())),
            preferred_element_type=jnp.float32,
        )
        for i, (slot, j) in enumerate(pieces):
            by_real = products[2 * PIECE * i : 2 * PIECE * i + PIECE]
            by_imag = products[2 * PIECE * i + PIECE : 2 * PIECE * (i + 1)]
            parts = []
            for r in range(C):
                at_real, at_imag = slice(256 * r, 256 * r + 128), slice(256 * r + 128, 256 * (r + 1))
                parts.append(by_real[:, at_real] - by_imag[:, at_imag])
                parts.append(by_imag[:, at_real] + by_real[:, at_imag])
            xsend[slot, j] = jnp.concatenate(
                [part[8 * h : 8 * (h + 1)] for h in range(2) for part in parts], axis=0
            ).astype(jnp.bfloat16)

            @pl.when(slot != mine)
            def _():
                owner = lax.rem(y + slot, Y)
                pltpu.make_async_remote_copy(
                    src_ref=xsend.at[slot, j],
                    dst_ref=xin.at[j, lax.rem(x - owner + X, X) - 1],
                    send_sem=x_send,
                    recv_sem=x_recv.at[j],
                    device_id={"x": owner},
                    device_id_type=MESH,
                ).start()

    def sum_over_x(slot, j):
        @pl.when(slot == mine)
        def _():
            pltpu.make_async_copy(xin.at[j], xin.at[j], x_recv.at[j]).wait()
            total = xsend[slot, j].astype(jnp.float32)
            for d in range(X - 1):
                total = total + xin[j, d].astype(jnp.float32)
            zsend[j] = total.astype(jnp.bfloat16)
            for h in range(2):
                target = 2 * by_core([PAIRS[k][j] for k in range(C)]) + h
                for r in range(C):

                    @pl.when(jnp.logical_or(target != z, c != r))
                    def _():
                        pltpu.make_async_remote_copy(
                            src_ref=zsend.at[j, pl.ds(32 * h + 16 * r, 16)],
                            dst_ref=zbuf.at[lax.rem(z - target + Z, Z)],
                            send_sem=z_send,
                            recv_sem=z_recv,
                            device_id={"z": target, "c": r},
                            device_id_type=MESH,
                        ).start()

    def pair(j):
        multiply(kbuf[j, 1:3].reshape(4 * PIECE, depth), [(UP, j), (DOWN, j)])

    def far(j):
        arrived(FAR, j)
        multiply(kbuf[j, 0], [(FAR, j)])

    @pl.when(c == 0)
    def _():
        pl.semaphore_wait(known.at[RELAY], 2)
        tell(X_KNOWN, c=1)

    @pl.when(c == 1)
    def _():
        pl.semaphore_wait(known.at[X_KNOWN], 1)

    multiply(own[...].reshape(8 * PIECE, depth), [(OWN, j) for j in range(PIECES)])

    pair(0)

    def hear_z():
        pl.semaphore_wait(barrier, 2 * (Z - 1))
        tell(Z_KNOWN, c=0)

    pl.when(jnp.logical_and(c == 1, z >= 8))(hear_z)

    def know_z():
        @pl.when(jnp.logical_and(c == 1, z < 8))
        def _():
            hear_z()

        @pl.when(c == 0)
        def _():
            pl.semaphore_wait(known.at[Z_KNOWN], 1)

    def sums(*which):
        for slot, j in which:
            sum_over_x(slot, j)

    early = z < EARLY

    def first_sums():
        sums((OWN, 0), (UP, 0), (DOWN, 0))

    def second_sums():
        sums((FAR, 0))

    def third_sums():
        sums((OWN, 1), (UP, 1), (DOWN, 1), (OWN, 2), (OWN, 3))

    pair_arrived(1)
    send_own(3)
    far(0)
    pair(1)

    @pl.when(jnp.logical_not(early))
    def _():
        know_z()
        first_sums()

    pair_arrived(2)

    @pl.when(jnp.logical_not(early))
    def _():
        second_sums()

    pair(2)
    far(1)
    pair_arrived(3)

    @pl.when(jnp.logical_not(early))
    def _():
        third_sums()

    pair(3)

    @pl.when(early)
    def _():
        know_z()
        first_sums()
        second_sums()
        third_sums()

    far(2)
    sums((UP, 2), (DOWN, 2), (FAR, 1))
    far(3)
    sums((UP, 3), (DOWN, 3), (FAR, 2), (FAR, 3))

    for copy in u_copies:
        copy.wait_send()
    pltpu.make_async_copy(given, given, give_send).wait()
    pltpu.make_async_copy(kbuf, kbuf, y_send).wait()
    pltpu.make_async_copy(xin, xin, x_send).wait()

    @pl.when(c == core_of_z)
    def _():
        sent = zbuf.at[pl.ds(1, Z - 1)]
        pltpu.make_async_copy(sent, sent, z_send).wait()

    @pl.when(c != core_of_z)
    def _():
        pltpu.make_async_copy(zbuf, zbuf, z_send).wait()

    @pl.when(c == core_of_z)
    def _():
        others = zbuf.at[pl.ds(1, Z - 1)]
        pltpu.make_async_copy(others, others, z_recv).wait()
        here = 32 * (z % 2) + 16 * c
        total = zsend[number_of_z, pl.ds(pl.multiple_of(here, 16), 16)].astype(jnp.float32)
        for d in range(1, Z):
            total = total + zbuf[d].astype(jnp.float32)
        out_ref[...] = total

    @pl.when(c != core_of_z)
    def _():
        pltpu.make_async_copy(zbuf, zbuf, z_recv).wait()
        total = zbuf[0].astype(jnp.float32)
        for d in range(1, Z):
            total = total + zbuf[d].astype(jnp.float32)
        out_ref[...] = total


def on_device(u_real, u_imag, psi_real, psi_imag, kick_angle, excited):
    rows, depth = u_real.shape
    bf16, f32 = jnp.bfloat16, jnp.float32
    any_place = pl.BlockSpec(memory_space=pl.ANY)
    vmem = pl.BlockSpec(memory_space=pltpu.VMEM)
    dma = pltpu.SemaphoreType.DMA
    out = pl.pallas_call(
        kernel,
        out_shape=pltpu.VMEM((16, rows), f32),
        in_specs=[any_place] * 6,
        out_specs=vmem,
        scratch_shapes=[
            pltpu.VMEM((1, 64), f32),
            pltpu.VMEM((1, depth), jnp.int32),
            pltpu.VMEM((2, 64, depth), bf16),
            pltpu.VMEM((C, 2, rows, depth), bf16),
            pltpu.VMEM((128, depth), bf16),
            pltpu.VMEM((128, 128), bf16),
            pltpu.VMEM((PIECES, 2 * PIECE, depth), bf16),
            pltpu.VMEM((2, 2 * PIECE, depth), bf16),
            pltpu.VMEM((PIECES, 3, 2 * PIECE, depth), bf16),
            pltpu.VMEM((Y, PIECES, 64, rows), bf16),
            pltpu.VMEM((PIECES, X - 1, 64, rows), bf16),
            pltpu.VMEM((PIECES, 64, rows), bf16),
            pltpu.VMEM((Z, 16, rows), bf16),
            dma((4,)),
            dma((2,)),
            dma((2,)),
            dma((2,)),
            dma,
            dma((PIECES,)),
            dma,
            dma((Y, PIECES)),
            dma,
            dma((PIECES,)),
            dma,
            dma,
            pltpu.SemaphoreType.REGULAR((4,)),
        ],
        compiler_params=pltpu.CompilerParams(
            collective_id=0, has_side_effects=True, vmem_limit_bytes=56 << 20
        ),
        cost_estimate=pl.CostEstimate(
            flops=4 * 2 * 256 * 256 * depth, bytes_accessed=6 * rows * depth * 2, transcendentals=0
        ),
    )(kick_angle[None, :], excited[None, :], psi_real.T, psi_imag.T, u_real, u_imag)
    return out[:8], out[8:]


def solution(mesh):
    split = Mesh(mesh.devices.reshape(Y, C, X, Z), ("y", "c", "x", "z"))
    return jax.shard_map(
        on_device,
        mesh=split,
        in_specs=(
            P(NARROW, WIDE),
            P(NARROW, WIDE),
            P(WIDE, NARROW),
            P(WIDE, NARROW),
            P(NARROW),
            P(WIDE),
        ),
        out_specs=(P(WIDE, NARROW), P(WIDE, NARROW)),
        check_vma=False,
    )
```
